32 devices in a mesh: gx: 8 (over z, core), gy: 4 (over y, x).
Axes of the slice: x: 2, y: 2, z: 4, core: 2. Of those that a mesh axis runs over, the one named last changes fastest.
Arguments:
- velocity: float32 [3, 2048, 512], P(None, 'gx', 'gy'), may hold values from 0.4 to 1.6
- adjoint_seed: float32 [3, 2048, 512], P(None, 'gx', 'gy'), may hold values from -6 to 6
- courant: float32 [3, 2048, 512], P(None, 'gx', 'gy'), may hold values from 0.1 to 0.45
- viscosity: float32 [3, 2048, 512], P(None, 'gx', 'gy'), may hold values from 0.02 to 0.1
- turbine_tile: int32 [128, 1], P(('gx', 'gy')), may hold values from 0 to 31; in each aligned block of 128 rows (0 to 127, 128 to 255, ...) at most 12 rows name the same one
- turbine_offset: int32 [128, 2], P(('gx', 'gy')), may hold values from 0 to 64
- thrust: float32 [128], P(('gx', 'gy')), may hold values from 0.5 to 2
- disk_width: float32 [128], P(('gx', 'gy')), may hold values from 8 to 16
Outputs:
- adjoint_start: float32 [3, 2048, 512], P(None, 'gx', 'gy')
- thrust_grad: float32 [128], P(('gx', 'gy'))
The draws below stay inside these ranges and needn't reach their ends.
Inputs may be any that keep to these rules, and one draw needn't show every extreme that they name: `turbine_tile`: each turbine's tile is the index along gx times the number of devices of gy plus the index along gy of the device whose cells hold its footprint. No tile holds more than 12 turbines, and some tile holds exactly 12.
All inputs are finite; a program needn't handle non-finite values.
Results may differ from the reference program's by a relative error of at most 0.00002.
Values sent between devices are 32-bit elements; how exact they have to be, the bound alone decides.
No kernel may reach another device: no remote copies, remote signals or barrier semaphores. Data moves between devices by JAX's collectives and lax.ppermute only.
A program may use at most 128 MiB of HBM per device.

```python
import math
import jax
import jax.numpy as jnp
import numpy as np
from jax import lax

LEV = 3
CX = 256
CY = 128
STEPS = 8
FP = 64
MOST = 12
NX = 2048
NY = 512
TURBINES = 128
N_GY = 4
DEVICES = 32


def plant(result, key, least, top_value):
    spot = [jax.random.randint(jax.random.fold_in(key, axis), (), 0, length) for axis, length in enumerate(result.shape)]
    widest = result.shape.index(max(result.shape))
    neighbour = spot[:widest] + [(spot[widest] + 1) % result.shape[widest]] + spot[widest + 1:]
    return result.at[tuple(spot)].set(least).at[tuple(neighbour)].set(top_value)


def block_levels(rng, dims, shards, least, largest):
    def one(axis_at, parts):
        steps = jax.random.uniform(jax.random.fold_in(jax.random.fold_in(rng, 6), axis_at), (parts,), jnp.float32, least / len(shards), largest / len(shards))
        return jnp.repeat(jnp.exp(steps), dims[axis_at] // parts).reshape((-1,) + (1,) * (len(dims) - axis_at - 1))

    gain = one(*shards[0])
    for cut in shards[1:]:
        gain = gain * one(*cut)
    return gain


def routed_block(key, own, number, rows, amount, top, most, lean):
    order = jax.random.permutation(key, amount)
    crowded, ordinary = portions_of(amount, rows * top, most, lean, True), portions_of(amount, rows * top, most, lean, False)
    places = jnp.arange(amount)

    def named(lengths, offset_by):
        used = int((lengths > 0).sum())
        fixed = max(1, used // 4)
        passed = fixed + (places - fixed + offset_by * (used - fixed)) % max(1, amount - fixed)
        return jnp.zeros((amount,), jnp.int32).at[order[jnp.where(places < fixed, places, passed)]].set(jnp.asarray(lengths, jnp.int32))

    lengths = jnp.where(number % 4 == 0, named(crowded, number // 4), named(ordinary, number - number // 4 - 1))
    mixed = jax.random.permutation(jax.random.fold_in(own, 3), amount)
    donor, sink = mixed[0:amount // 2 * 2:2], mixed[1:amount // 2 * 2:2]
    margin = jnp.minimum(lengths[donor] - 1, most - lengths[sink]) // 2
    margin = jnp.where((donor == order[0]) | (sink == order[0]) | (lengths[sink] == 0), 0, jnp.maximum(margin, 0))
    passed = jax.random.randint(jax.random.fold_in(own, 4), (amount // 2,), 0, 1 << 20) % (margin + 1)
    lengths = lengths.at[donor].add(-passed).at[sink].add(passed)
    items = jnp.searchsorted(jnp.cumsum(lengths), jnp.arange(rows * top), side="right").astype(jnp.int32)
    table = items.reshape(top, rows).T
    table = table[jax.random.permutation(jax.random.fold_in(own, 1), rows)]
    offset_by = jax.random.randint(jax.random.fold_in(own, 2), (rows, 1), 0, top)
    return jnp.take_along_axis(table, (jnp.arange(top)[None, :] + offset_by) % top, axis=1)


def portions_of(amount, total, limit, skew, full):
    portions = [(1 << 20) // math.isqrt(standing ** skew) + 1 for standing in range(1, amount + 1)]
    largest = limit if full else min(limit, max(-(-total // amount), total * portions[0] // sum(portions)))
    least = 1 if total - largest >= amount - 1 else 0
    counts, rest = [largest] + [least] * (amount - 1), total - largest - least * (amount - 1)
    while rest > 0:
        movable = [i for i in range(1, amount) if counts[i] < largest] or [i for i in range(1, amount) if counts[i] < limit]
        whole, budget = sum([portions[i] for i in movable]), rest
        for i in movable:
            extra = min(limit - counts[i], max(1, budget * portions[i] // whole), rest)
            counts[i] = counts[i] + extra
            rest = rest - extra
    return np.array(counts)


def gaussian(stream_key, shape, width, reach, cuts=(), kind=jnp.bfloat16):
    drawn = jax.random.normal(stream_key, shape, jnp.float32) * width
    if len(cuts) > 0:
        drawn = block_levels(stream_key, shape, cuts, -0.22, 0.18) * drawn
    return jnp.clip(drawn, min=-reach, max=reach).astype(kind)


def setup_inputs(seed: int = 0) -> dict:
    key_of = jax.random.split(jax.random.key(seed), 9)
    velocity = jnp.clip(0.4 + 1.2 * jax.random.uniform(key_of[0], (LEV, NX, NY), jnp.float32) ** block_levels(key_of[0], (LEV, NX, NY), ((1, 8), (2, 4)), -0.2, 0.2), 0.4, 1.6)
    adjoint_seed = gaussian(key_of[1], (LEV, NX, NY), 1.0, 6.0, ((1, 8), (2, 4)), jnp.float32)
    courant = jnp.clip(0.1 + 0.35 * jax.random.uniform(key_of[2], (LEV, NX, NY), jnp.float32) ** block_levels(key_of[2], (LEV, NX, NY), ((1, 8), (2, 4)), -0.2, 0.2), 0.1, 0.45)
    viscosity = jnp.clip(0.02 + 0.08 * jax.random.uniform(key_of[3], (LEV, NX, NY), jnp.float32) ** block_levels(key_of[3], (LEV, NX, NY), ((1, 8), (2, 4)), -0.2, 0.2), 0.02, 0.1)
    turbine_tile_keys = jax.random.split(jax.random.fold_in(key_of[4], 1), TURBINES // TURBINES)
    turbine_tile_turns = jax.random.permutation(jax.random.fold_in(key_of[4], 3), TURBINES // TURBINES)
    turbine_tile = jax.vmap(lambda own, number: routed_block(jax.random.fold_in(key_of[4], 2), own, number, TURBINES, DEVICES, 1, MOST, 2))(turbine_tile_keys, turbine_tile_turns).reshape((TURBINES, 1))
    turbine_offset = plant(jax.random.randint(key_of[5], (TURBINES, 2), 0, min(CX, CY) - FP + 1), jax.random.fold_in(key_of[5], 1), 0, min(CX, CY) - FP).astype(jnp.int32)
    thrust = jnp.clip(jnp.exp(math.log(2.0) - 1.3862944 * jax.random.uniform(key_of[6], (TURBINES,), jnp.float32) ** block_levels(key_of[6], (TURBINES,), ((0, 32),), -0.2, 0.2)), 0.5, 2.0)
    disk_width = jnp.clip(jnp.exp(math.log(16.0) - 0.6931472 * jax.random.uniform(key_of[7], (TURBINES,), jnp.float32) ** block_levels(key_of[7], (TURBINES,), ((0, 32),), -0.2, 0.2)), 8.0, 16.0)
    return dict(velocity=velocity, adjoint_seed=adjoint_seed, courant=courant, viscosity=viscosity, turbine_tile=turbine_tile, turbine_offset=turbine_offset, thrust=thrust, disk_width=disk_width)


VERTICAL_MIX = 0.05
DRAG_SCALE = 0.01

def drag_law(state):
    return state * jnp.sqrt(state * state + 1.0)

def drag_slope(state):
    square_one = state * state + 1.0
    return (square_one + state * state) / jnp.sqrt(square_one)

def vertical(center):
    zero_row = jnp.zeros_like(center[:1])
    from_above = jnp.concatenate([center[1:] - center[:-1], zero_row], axis=0)
    from_below = jnp.concatenate([zero_row, center[:-1] - center[1:]], axis=0)
    return from_above + from_below

def advance(padded, advect, diffuse, drag_coef):
    center = padded[:, 1:-1, 1:-1]
    upwind = padded[:, :-2, 1:-1]
    downwind = padded[:, 2:, 1:-1]
    left_cell = padded[:, 1:-1, :-2]
    right_cell = padded[:, 1:-1, 2:]
    return center + advect * (upwind - center) + diffuse * (downwind + upwind + right_cell + left_cell - 4.0 * center) + VERTICAL_MIX * vertical(center) - drag_coef * drag_law(center)

def retreat(padded, advect_ext, diffuse_ext, drag_coef, state):
    flux_adv = advect_ext * padded
    flux_dif = diffuse_ext * padded
    center = padded[:, 1:-1, 1:-1]
    return center - flux_adv[:, 1:-1, 1:-1] - 4.0 * flux_dif[:, 1:-1, 1:-1] + flux_adv[:, 2:, 1:-1] + (flux_dif[:, 2:, 1:-1] + flux_dif[:, :-2, 1:-1] + flux_dif[:, 1:-1, 2:] + flux_dif[:, 1:-1, :-2]) + VERTICAL_MIX * vertical(center) - drag_coef * drag_slope(state) * center

def footprint(disk_width):
    cell_pos = jnp.arange(FP, dtype=jnp.float32) - (FP - 1) / 2.0
    profile = jnp.exp(-(cell_pos[None, :] * cell_pos[None, :]) / (2.0 * disk_width[:, None] * disk_width[:, None]))
    level_pos = jnp.arange(LEV, dtype=jnp.float32) - (LEV - 1) / 2.0
    level_gain = DRAG_SCALE * jnp.exp(-0.5 * level_pos * level_pos)
    return level_gain[None, :, None, None] * profile[:, None, :, None] * profile[:, None, None, :]

def wrap_pad(array):
    return jnp.pad(array, ((0, 0), (1, 1), (1, 1)), mode='wrap')

def reference(velocity, adjoint_seed, courant, viscosity, turbine_tile, turbine_offset, thrust, disk_width):
    tile_ids = turbine_tile[:, 0]
    row_start = (tile_ids // N_GY * CX + turbine_offset[:, 0]).astype(jnp.int32)
    col_start = (tile_ids % N_GY * CY + turbine_offset[:, 1]).astype(jnp.int32)
    kernels = footprint(disk_width)

    def add_turbine(turbine, field_now):
        corner = (jnp.int32(0), row_start[turbine], col_start[turbine])
        block_vals = lax.dynamic_slice(field_now, corner, (LEV, FP, FP))
        return lax.dynamic_update_slice(field_now, block_vals + thrust[turbine] * kernels[turbine], corner)
    drag_field = lax.fori_loop(0, TURBINES, add_turbine, jnp.zeros((LEV, NX, NY), jnp.float32))
    states = []
    state = velocity
    for step_index in range(STEPS):
        states.append(state)
        if step_index + 1 < STEPS:
            state = advance(wrap_pad(state), courant, viscosity, drag_field)
    advect_ext = wrap_pad(courant)
    diffuse_ext = wrap_pad(viscosity)
    adjoint = adjoint_seed
    sensitivity = jnp.zeros((LEV, NX, NY), jnp.float32)
    for step_index in reversed(range(STEPS)):
        sensitivity = sensitivity - adjoint * drag_law(states[step_index])
        adjoint = retreat(wrap_pad(adjoint), advect_ext, diffuse_ext, drag_field, states[step_index])

    def turbine_total(turbine):
        corner = (jnp.int32(0), row_start[turbine], col_start[turbine])
        block_vals = lax.dynamic_slice(sensitivity, corner, (LEV, FP, FP))
        return jnp.sum(kernels[turbine] * block_vals)
    totals = lax.map(turbine_total, jnp.arange(TURBINES, dtype=jnp.int32))
    return (adjoint, thrust * totals)
```

```python
import functools
import math

import jax
import jax.numpy as jnp
from jax import lax
from jax.experimental import pallas as pl
from jax.experimental.pallas import tpu as pltpu
from jax.sharding import PartitionSpec as P

STEPS = 8
FP = 64
VERTICAL_MIX = 0.05
DRAG_SCALE = 0.01
SIDE_GAIN = math.exp(-0.5)

LEV, CX, CY = 3, 256, 128
WIDE = 14
MID = 13
THIN = 8
GAP = 42
RIM = 16
TOP = 24
TALL = CX + 2 * TOP
SIDE_ROWS = CX + 64
END_ROWS = 3 * LEV * RIM + LEV * THIN + 2 * RIM + 2 * THIN
VALUES = 6
FORWARD_ROWS = 32
ADJOINT_ROWS = 32


def lane_ids():
    return lax.broadcasted_iota(jnp.int32, (1, CY), 1)


def spread_lanes(value, rows):
    return jnp.broadcast_to(value, (rows, CY))


def rolled(value, shift):
    shift = shift % CY
    return value if shift == 0 else pltpu.roll(value, shift, 1)


def rim_place(lane):
    level = jnp.where((lane >= GAP // 2) & (lane < GAP // 2 + GAP), 1, 0)
    level = jnp.where((lane >= GAP // 2 + GAP) & (lane < GAP // 2 + 2 * GAP), 2, level)
    place = lane - GAP * level
    place = jnp.where(lane >= GAP // 2 + 2 * GAP, lane - CY, place)
    return level, place


def for_rows(first, count, chunk, body):
    full = count // chunk
    if full == 1:
        body(first, chunk)
    elif full > 1:

        def one(index, carry):
            body(pl.multiple_of(first + index * chunk, 8), chunk)
            return carry

        lax.fori_loop(0, full, one, 0)
    if count > full * chunk:
        body(first + full * chunk, count - full * chunk)


def pack_sides(
    n_gy, tile_ref, offset_ref, thrust_ref, width_ref, vel_ref, seed_ref, cou_ref, vis_ref,
    up_ref, down_ref, info_ref,
):
    lane = lane_ids()
    whole = jnp.zeros((1, CY), jnp.int32)
    real = jnp.zeros((1, CY), jnp.float32)
    for k in range(thrust_ref.shape[0]):
        tile = tile_ref[k, 0]
        for spot, value in enumerate(
            (tile // n_gy, tile % n_gy, offset_ref[k, 0], offset_ref[k, 1])
        ):
            whole = jnp.where(lane == VALUES * k + spot, value, whole)
        real = jnp.where(lane == VALUES * k + 4, thrust_ref[k], real)
        real = jnp.where(lane == VALUES * k + 5, width_ref[k], real)
    info_ref[...] = jnp.broadcast_to(whole.astype(jnp.float32) + real, info_ref.shape)

    for out_ref, low in ((up_ref, False), (down_ref, True)):

        def one(first, rows, out_ref=out_ref, low=low):
            total = jnp.zeros((rows, CY), jnp.float32)
            start = 0
            for ref, width in ((vel_ref, WIDE), (cou_ref, MID), (vis_ref, MID)):
                for level in range(LEV):
                    to = GAP * level + start
                    moved = rolled(
                        ref[level, pl.ds(first, rows), :], to - (0 if low else CY - width)
                    )
                    total = jnp.where((lane >= to) & (lane < to + width), moved, total)
                start += width
            out_ref[pl.ds(first, rows), :] = total

        for_rows(0, CX, 32, one)
        total = jnp.zeros((64, CY), jnp.float32)
        for block in range(4):
            for level in range(LEV):
                to = 32 * block + THIN * level
                moved = rolled(
                    seed_ref[level, 64 * block : 64 * block + 64, :],
                    to - (0 if low else CY - THIN),
                )
                total = jnp.where((lane >= to) & (lane < to + THIN), moved, total)
        out_ref[CX:SIDE_ROWS, :] = total


def pack_ends(west_ref, east_ref, vel_ref, seed_ref, cou_ref, vis_ref, up_ref, down_ref):
    for out_ref, low in ((up_ref, False), (down_ref, True)):
        at = 0
        first = 0 if low else CX - RIM
        for ref in (vel_ref, cou_ref, vis_ref):
            for level in range(LEV):
                out_ref[at : at + RIM, :] = ref[level, first : first + RIM, :]
                at += RIM
        thin_first = 0 if low else CX - THIN
        for level in range(LEV):
            out_ref[at : at + THIN, :] = seed_ref[level, thin_first : thin_first + THIN, :]
            at += THIN
        for ref in (west_ref, east_ref):
            out_ref[at : at + RIM, :] = ref[first : first + RIM, :]
            at += RIM
        side_first = CX if low else SIDE_ROWS - THIN
        for ref in (west_ref, east_ref):
            out_ref[at : at + THIN, :] = ref[side_first : side_first + THIN, :]
            at += THIN


def window(
    n_gx, n_gy, per_device,
    place_ref, info_ref, vel_ref, seed_ref, cou_ref, vis_ref, west_ref, east_ref, low_ref, high_ref,
    start_ref, grads_ref,
    u_buf, l_buf, g_buf, f_buf, a_buf, w_buf, v_buf, d_buf, s_buf, rows_buf, cols_buf,
):
    lane = lane_ids()
    level_of, place = rim_place(lane)
    west_lane, east_lane = place == -1, place == 0
    level_one, level_two = level_of == 1, level_of == 2
    valid = (place >= -WIDE) & (place < WIDE)
    from_above = jnp.where(valid & (level_of < LEV - 1), VERTICAL_MIX, 0.0).astype(jnp.float32)
    from_below = jnp.where(valid & (level_of > 0), VERTICAL_MIX, 0.0).astype(jnp.float32)
    rim_mix = from_above + from_below
    first_lane, last_lane = lane == 0, lane == CY - 1

    devices = info_ref.shape[0]
    my_gx = place_ref[0].astype(jnp.float32)
    my_gy = place_ref[1].astype(jnp.float32)
    col_of = jnp.where(place < 0, place, CY + place).astype(jnp.float32)
    row_lane = lax.broadcasted_iota(jnp.int32, (1, 3 * CY), 1).astype(jnp.float32)
    row_profiles, rim_profiles = [], []

    def near(delta, count):
        delta = jnp.where(delta >= count / 2, delta - count, delta)
        return jnp.where(delta < -count / 2, delta + count, delta)

    def profile(cells, first, width):
        at = cells - first
        centred = at - (FP - 1) / 2.0
        value = jnp.exp(-(centred * centred) / (2.0 * width * width))
        return jnp.where((at >= 0.0) & (at < float(FP)), value, 0.0)

    for k in range(per_device):
        info = info_ref[:, VALUES * k : VALUES * k + VALUES]
        row_first = near(info[:, 0:1] - my_gx, n_gx) * CX + info[:, 2:3]
        col_first = near(info[:, 1:2] - my_gy, n_gy) * CY + info[:, 3:4]
        scale = DRAG_SCALE * info[:, 4:5]
        width = info[:, 5:6]
        part = pl.ds(k * devices, devices)
        row_profiles.append(profile(row_lane - RIM, row_first, width) * scale)
        rows_buf[part, :] = profile(row_lane[:, :CX], row_first, width) * scale
        cols_buf[part, :] = profile(lane.astype(jnp.float32), col_first, width)
        rim_profiles.append(profile(col_of, col_first, width))
    along_rows = jnp.concatenate(row_profiles, axis=0)
    along_cols = jnp.concatenate([cols_buf[...], jnp.concatenate(rim_profiles, axis=0)], axis=1)
    drag = lax.dot_general(
        along_rows.T, along_cols, (((1,), (0,)), ((), ())),
        precision=lax.Precision.HIGHEST, preferred_element_type=jnp.float32,
    )
    tall = pl.ds(TOP - RIM, CX + 2 * RIM)
    gain = jnp.where(valid, jnp.where(level_one, 1.0, SIDE_GAIN), 0.0).astype(jnp.float32)
    d_buf[0, tall, :] = drag[: CX + 2 * RIM, :CY]
    d_buf[1, tall, :] = drag[: CX + 2 * RIM, :CY] * SIDE_GAIN
    d_buf[2, tall, :] = drag[: CX + 2 * RIM, CY:] * gain

    edge = jnp.zeros((TOP - RIM, CY), jnp.float32)
    for tile in range(LEV + 1):
        for buf in (a_buf, w_buf, v_buf):
            buf[tile, 0 : TOP - RIM, :] = edge
            buf[tile, TALL - TOP + RIM :, :] = edge
        for buf in (u_buf, l_buf):
            for slot in range(2):
                buf[slot, tile, 0 : TOP - RIM, :] = edge
                buf[slot, tile, TALL - TOP + RIM :, :] = edge
        for slot in range(2):
            l_buf[slot, tile, TOP - RIM : TOP - THIN, :] = edge
            l_buf[slot, tile, TOP + CX + THIN : TOP + CX + RIM, :] = edge

    def coefficients(tile, to, rows, courant, viscosity, mix):
        a_buf[tile, pl.ds(to, rows), :] = 1.0 - courant - 4.0 * viscosity - mix
        w_buf[tile, pl.ds(to, rows), :] = courant + viscosity
        v_buf[tile, pl.ds(to, rows), :] = viscosity

    def level_mix(level):
        return VERTICAL_MIX * (2 if level == 1 else 1)

    def rim(west, east, to, rows):
        zero = jnp.zeros((rows, CY), jnp.float32)
        start = 0
        found = []
        for width in (WIDE, MID, MID):
            value = jnp.where((place >= 0) & (place < width), rolled(east, -start), zero)
            found.append(
                jnp.where((place >= -width) & (place < 0), rolled(west, -start - width), value)
            )
            start += width
        u_buf[0, LEV, pl.ds(to, rows), :] = found[0]
        coefficients(LEV, to, rows, found[1], found[2], rim_mix)

    def thin_rim(west, east, block, to, rows):
        value = jnp.zeros((rows, CY), jnp.float32)
        for level in range(LEV):
            at = GAP * level - (32 * block + THIN * level)
            mine = level_of == level
            value = jnp.where(mine & (place >= 0) & (place < THIN), rolled(east, at), value)
            value = jnp.where(mine & (place >= -THIN) & (place < 0), rolled(west, at - THIN), value)
        l_buf[0, LEV, pl.ds(to, rows), :] = value

    def load_core(first, rows):
        for level in range(LEV):
            at = pl.ds(first, rows)
            u_buf[0, level, pl.ds(first + TOP, rows), :] = vel_ref[level, at, :]
            l_buf[0, level, pl.ds(first + TOP, rows), :] = seed_ref[level, at, :]
            coefficients(
                level, first + TOP, rows, cou_ref[level, at, :], vis_ref[level, at, :], level_mix(level)
            )
        rim(west_ref[pl.ds(first, rows), :], east_ref[pl.ds(first, rows), :], first + TOP, rows)

    for_rows(0, CX, 32, load_core)
    for block in range(4):
        at = pl.ds(CX, 64)
        thin_rim(west_ref[at, :], east_ref[at, :], block, TOP + 64 * block, 64)
    for ref, to, thin_to, block in (
        (low_ref, TOP - RIM, TOP - THIN, 3),
        (high_ref, TOP + CX, TOP + CX, 0),
    ):
        for level in range(LEV):
            u_buf[0, level, to : to + RIM, :] = ref[RIM * level : RIM * level + RIM, :]
            courant = ref[RIM * (LEV + level) : RIM * (LEV + level) + RIM, :]
            viscosity = ref[RIM * (2 * LEV + level) : RIM * (2 * LEV + level) + RIM, :]
            coefficients(level, to, RIM, courant, viscosity, level_mix(level))
            at = 3 * LEV * RIM + THIN * level
            l_buf[0, level, thin_to : thin_to + THIN, :] = ref[at : at + THIN, :]
        at = 3 * LEV * RIM + LEV * THIN
        rim(ref[at : at + RIM, :], ref[at + RIM : at + 2 * RIM, :], to, RIM)
        at += 2 * RIM
        thin_rim(ref[at : at + THIN, :], ref[at + THIN : at + 2 * THIN, :], block, thin_to, THIN)

    def sideways(core, packed):
        sums = []
        for level in range(LEV):
            other = rolled(packed, -GAP * level)
            left = rolled(jnp.where(last_lane, other, core[level]), 1)
            right = rolled(jnp.where(first_lane, other, core[level]), -1)
            sums.append(left + right)
        other = jnp.where(level_one, rolled(core[1], GAP), core[0])
        other = jnp.where(level_two, rolled(core[2], 2 * GAP), other)
        left = rolled(jnp.where(west_lane, other, packed), 1)
        right = rolled(jnp.where(east_lane, other, packed), -1)
        sums.append(left + right)
        return sums

    def upright(core, packed):
        middle = VERTICAL_MIX * core[1]
        mixed = [middle, VERTICAL_MIX * (core[0] + core[2]), middle]
        if packed is not None:
            mixed.append(from_above * rolled(packed, -GAP) + from_below * rolled(packed, GAP))
        return mixed

    def drag_of(tile, at):
        return d_buf[(1, 0, 1, 2)[tile], at, :]

    def drag_terms(state, drag_here):
        square = state * state + 1.0
        root = lax.rsqrt(square)
        weak = drag_here * root
        return square, root, weak, weak * square

    for step in range(STEPS - 1):
        rows_beyond = RIM if STEPS + 5 - step > 8 else 8
        now, later = step % 2, (step + 1) % 2

        def advance(first, rows, step=step, now=now, later=later):
            at = pl.ds(first, rows)
            state = [u_buf[now, tile, at, :] for tile in range(LEV + 1)]
            sides = sideways(state[:LEV], state[LEV])
            mixed = upright(state[:LEV], state[LEV])
            for tile in range(LEV + 1):
                upwind = u_buf[now, tile, pl.ds(first - 1, rows), :]
                downwind = u_buf[now, tile, pl.ds(first + 1, rows), :]
                square, root, weak, strong = drag_terms(state[tile], drag_of(tile, at))
                centre = a_buf[tile, at, :] - strong
                u_buf[later, tile, at, :] = (
                    centre * state[tile]
                    + w_buf[tile, at, :] * upwind
                    + v_buf[tile, at, :] * (downwind + sides[tile])
                    + mixed[tile]
                )
                g_buf[step, tile, at, :] = centre - strong + weak
                if tile < LEV:
                    f_buf[step, tile, at, :] = state[tile] * (square * root)

        for_rows(TOP - rows_beyond, CX + 2 * rows_beyond, FORWARD_ROWS, advance)

    last = STEPS - 1

    def slopes(first, rows):
        at = pl.ds(first, rows)
        for tile in range(LEV + 1):
            state = u_buf[last % 2, tile, at, :]
            square, root, weak, strong = drag_terms(state, drag_of(tile, at))
            g_buf[last, tile, at, :] = a_buf[tile, at, :] - 2.0 * strong + weak
            if tile < LEV:
                f_buf[last, tile, at, :] = state * (square * root)

    for_rows(TOP - 8, CX + 16, FORWARD_ROWS, slopes)

    zero = jnp.zeros((CX + 16, CY), jnp.float32)
    for part in range(2):
        s_buf[part, TOP - 8 : TOP + CX + 8, :] = zero
    for step in reversed(range(STEPS)):
        rows_beyond = 8 if step else 0
        now, later = (last - step) % 2, (last - step + 1) % 2

        def retreat(first, rows, step=step, now=now, later=later):
            at = pl.ds(first, rows)
            before, after = pl.ds(first - 1, rows), pl.ds(first + 1, rows)
            adjoint = [l_buf[now, tile, at, :] for tile in range(LEV + 1)]
            flux = [v_buf[tile, at, :] * adjoint[tile] for tile in range(LEV + 1)]
            sides = sideways(flux[:LEV], flux[LEV])
            mixed = upright(adjoint[:LEV], adjoint[LEV] if step else None)
            for tile in range(LEV + 1 if step else LEV):
                value = (
                    g_buf[step, tile, at, :] * adjoint[tile]
                    + w_buf[tile, after, :] * l_buf[now, tile, after, :]
                    + v_buf[tile, before, :] * l_buf[now, tile, before, :]
                    + sides[tile]
                    + mixed[tile]
                )
                if step:
                    l_buf[later, tile, at, :] = value
                else:
                    start_ref[tile, pl.ds(first - TOP, rows), :] = value
            s_buf[0, at, :] += f_buf[step, 1, at, :] * adjoint[1]
            s_buf[1, at, :] += (
                f_buf[step, 0, at, :] * adjoint[0] + f_buf[step, 2, at, :] * adjoint[2]
            )

        for_rows(TOP - rows_beyond, CX + 2 * rows_beyond, ADJOINT_ROWS, retreat)

    inside = pl.ds(TOP, CX)
    sensitivity = s_buf[0, inside, :] + SIDE_GAIN * s_buf[1, inside, :]
    across = lax.dot_general(
        rows_buf[...], sensitivity, (((1,), (0,)), ((), ())),
        precision=lax.Precision.HIGHEST, preferred_element_type=jnp.float32,
    )
    sums = -jnp.sum(across * cols_buf[...], axis=1, keepdims=True)
    grads = jnp.zeros((devices, CY), jnp.float32)
    for k in range(per_device):
        mine = spread_lanes(sums[k * devices : (k + 1) * devices, :], devices)
        grads = jnp.where(lane == k, mine, grads)
    grads_ref[...] = grads


def shards(
    velocity, adjoint_seed, courant, viscosity, turbine_tile, turbine_offset, thrust, disk_width
):
    n_gx, n_gy = lax.axis_size("gx"), lax.axis_size("gy")
    devices = n_gx * n_gy
    per_device = thrust.shape[0]
    f32 = jnp.float32
    smem = pl.BlockSpec(memory_space=pltpu.SMEM)
    vmem = pl.BlockSpec(memory_space=pltpu.VMEM)

    def ring(axis, by):
        count = lax.axis_size(axis)
        return [(i, (i + by) % count) for i in range(count)]

    side_up, side_down, info = pl.pallas_call(
        functools.partial(pack_sides, n_gy),
        name="pack_sides",
        out_shape=(
            jax.ShapeDtypeStruct((SIDE_ROWS, CY), f32),
            jax.ShapeDtypeStruct((SIDE_ROWS, CY), f32),
            jax.ShapeDtypeStruct((devices, CY), f32),
        ),
        in_specs=[smem] * 4 + [vmem] * 4,
        out_specs=(vmem,) * 3,
    )(turbine_tile, turbine_offset, thrust, disk_width, velocity, adjoint_seed, courant, viscosity)
    west = lax.ppermute(side_up, "gy", ring("gy", 1))
    east = lax.ppermute(side_down, "gy", ring("gy", -1))
    info = lax.all_to_all(info, ("gx", "gy"), 0, 0, tiled=True)
    end_up, end_down = pl.pallas_call(
        pack_ends,
        name="pack_ends",
        out_shape=(jax.ShapeDtypeStruct((END_ROWS, CY), f32),) * 2,
        in_specs=[vmem] * 6,
        out_specs=(vmem,) * 2,
    )(west, east, velocity, adjoint_seed, courant, viscosity)
    low = lax.ppermute(end_up, "gx", ring("gx", 1))
    high = lax.ppermute(end_down, "gx", ring("gx", -1))
    place = jnp.stack([lax.axis_index("gx"), lax.axis_index("gy")]).astype(jnp.int32)
    turbines = devices * per_device
    adjoint_start, grads = pl.pallas_call(
        functools.partial(window, n_gx, n_gy, per_device),
        name="window",
        out_shape=(
            jax.ShapeDtypeStruct((LEV, CX, CY), f32),
            jax.ShapeDtypeStruct((devices, CY), f32),
        ),
        in_specs=[smem] + [vmem] * 9,
        out_specs=(vmem,) * 2,
        scratch_shapes=[
            pltpu.VMEM((2, LEV + 1, TALL, CY), f32),
            pltpu.VMEM((2, LEV + 1, TALL, CY), f32),
            pltpu.VMEM((STEPS, LEV + 1, TALL, CY), f32),
            pltpu.VMEM((STEPS, LEV, TALL, CY), f32),
            pltpu.VMEM((LEV + 1, TALL, CY), f32),
            pltpu.VMEM((LEV + 1, TALL, CY), f32),
            pltpu.VMEM((LEV + 1, TALL, CY), f32),
            pltpu.VMEM((3, TALL, CY), f32),
            pltpu.VMEM((2, TALL, CY), f32),
            pltpu.VMEM((turbines, CX), f32),
            pltpu.VMEM((turbines, CY), f32),
        ],
        compiler_params=pltpu.CompilerParams(vmem_limit_bytes=48 * 1024 * 1024),
    )(place, info, velocity, adjoint_seed, courant, viscosity, west, east, low, high)
    grads = lax.all_to_all(grads, ("gx", "gy"), 0, 0, tiled=True)
    return adjoint_start, jnp.sum(grads, axis=0)[:per_device]


def solution(mesh):
    tiled = P(None, "gx", "gy")
    spread = P(("gx", "gy"))
    matrix = P(("gx", "gy"), None)
    return jax.shard_map(
        shards,
        mesh=mesh,
        in_specs=(tiled, tiled, tiled, tiled, matrix, matrix, spread, spread),
        out_specs=(tiled, spread),
        check_vma=False,
    )
```

```python
import functools
import math

import jax
import jax.numpy as jnp
from jax import lax
from jax.experimental import pallas as pl
from jax.experimental.pallas import tpu as pltpu
from jax.sharding import PartitionSpec as P

STEPS = 8
FP = 64
VERTICAL_MIX = 0.05
DRAG_SCALE = 0.01
SIDE_GAIN = math.exp(-0.5)

LEV, CX, CY = 3, 256, 128
WIDE = 14
MID = 13
THIN = 8
GAP = 42
RIM = 16
TOP = 24
TALL = CX + 2 * TOP
SIDE_ROWS = CX + 64
END_ROWS = 3 * LEV * RIM + LEV * THIN + 2 * RIM + 2 * THIN
VALUES = 6
CHUNK = 32
AHEAD = 2
SMALL = pltpu.CompilerParams(vmem_limit_bytes=8 * 1024 * 1024)


def lane_ids():
    return lax.broadcasted_iota(jnp.int32, (1, CY), 1)


def spread_lanes(value, rows):
    return jnp.broadcast_to(value, (rows, CY))


def rolled(value, shift):
    shift = shift % CY
    return value if shift == 0 else pltpu.roll(value, shift, 1)


def rim_place(lane):
    level = jnp.where((lane >= GAP // 2) & (lane < GAP // 2 + GAP), 1, 0)
    level = jnp.where((lane >= GAP // 2 + GAP) & (lane < GAP // 2 + 2 * GAP), 2, level)
    place = lane - GAP * level
    place = jnp.where(lane >= GAP // 2 + 2 * GAP, lane - CY, place)
    return level, place


def for_rows(first, count, chunk, body):
    full = count // chunk
    if full == 1:
        body(first, chunk)
    elif full > 1:

        def one(index, carry):
            body(pl.multiple_of(first + index * chunk, 8), chunk)
            return carry

        lax.fori_loop(0, full, one, 0)
    if count > full * chunk:
        body(first + full * chunk, count - full * chunk)


def pack_sides(
    n_gy, tile_hbm, offset_hbm, thrust_hbm, width_hbm, vel_hbm, seed_hbm, cou_hbm, vis_hbm,
    up_ref, down_ref, info_ref,
    tile_ref, offset_ref, thrust_ref, width_ref, vel_ref, seed_ref, cou_ref, vis_ref, arrived,
):
    copies = [
        pltpu.make_async_copy(source, target, arrived.at[index])
        for index, (source, target) in enumerate(
            (
                (seed_hbm, seed_ref), (vel_hbm, vel_ref), (cou_hbm, cou_ref), (vis_hbm, vis_ref),
                (tile_hbm, tile_ref), (offset_hbm, offset_ref), (thrust_hbm, thrust_ref),
                (width_hbm, width_ref),
            )
        )
    ]
    for copy in copies:
        copy.start()
    lane = lane_ids()
    level_of, _ = rim_place(lane)
    for copy in copies[4:]:
        copy.wait()
    whole = jnp.zeros((1, CY), jnp.int32)
    real = jnp.zeros((1, CY), jnp.float32)
    for k in range(thrust_ref.shape[0]):
        tile = tile_ref[k]
        for spot, value in enumerate(
            (tile // n_gy, tile % n_gy, offset_ref[0, k], offset_ref[1, k])
        ):
            whole = jnp.where(lane == VALUES * k + spot, value, whole)
        real = jnp.where(lane == VALUES * k + 4, thrust_ref[k], real)
        real = jnp.where(lane == VALUES * k + 5, width_ref[k], real)
    info_ref[...] = jnp.broadcast_to(whole.astype(jnp.float32) + real, info_ref.shape)

    copies[0].wait()
    for out_ref, low in ((up_ref, False), (down_ref, True)):
        total = jnp.zeros((64, CY), jnp.float32)
        for block in range(4):
            for level in range(LEV):
                to = 32 * block + THIN * level
                moved = rolled(
                    seed_ref[level, 64 * block : 64 * block + 64, :],
                    to - (0 if low else CY - THIN),
                )
                total = jnp.where((lane >= to) & (lane < to + THIN), moved, total)
        out_ref[CX:SIDE_ROWS, :] = total

    def around(ref):
        value = jnp.where(level_of == 1, rolled(ref[1], GAP), ref[0])
        return jnp.where(level_of == 2, rolled(ref[2], 2 * GAP), value)

    up = down = None
    for index, (ref, width) in enumerate(((vel_ref, WIDE), (cou_ref, MID), (vis_ref, MID))):
        copies[1 + index].wait()
        both = around(ref)
        start = (0, WIDE, WIDE + MID)[index]
        if index == 0:
            up, down = rolled(both, width), both
        else:
            mine = in_share(lane, start, width)
            up = jnp.where(mine, rolled(both, start + width), up)
            down = jnp.where(mine, rolled(both, start), down)
    up_ref[0:CX, :] = up
    down_ref[0:CX, :] = down


def in_share(lane, start, width):
    inside = jnp.zeros(lane.shape, jnp.bool_)
    for level in range(LEV):
        first = GAP * level + start
        inside = inside | ((lane >= first) & (lane < first + width))
    return inside


def pack_ends(west_ref, east_ref, vel_ref, seed_ref, cou_ref, vis_ref, up_ref, down_ref):
    for out_ref, low in ((up_ref, False), (down_ref, True)):
        at = 0
        first = 0 if low else CX - RIM
        for ref in (vel_ref, cou_ref, vis_ref):
            for level in range(LEV):
                out_ref[at : at + RIM, :] = ref[level, first : first + RIM, :]
                at += RIM
        thin_first = 0 if low else CX - THIN
        for level in range(LEV):
            out_ref[at : at + THIN, :] = seed_ref[level, thin_first : thin_first + THIN, :]
            at += THIN
        for ref in (west_ref, east_ref):
            out_ref[at : at + RIM, :] = ref[first : first + RIM, :]
            at += RIM
        side_first = CX if low else SIDE_ROWS - THIN
        for ref in (west_ref, east_ref):
            out_ref[at : at + THIN, :] = ref[side_first : side_first + THIN, :]
            at += THIN


def level_mix(level):
    return VERTICAL_MIX * (2 if level == 1 else 1)


def rim_mixes():
    level_of, place = rim_place(lane_ids())
    valid = (place >= -WIDE) & (place < WIDE)
    from_above = jnp.where(valid & (level_of < LEV - 1), VERTICAL_MIX, 0.0).astype(jnp.float32)
    from_below = jnp.where(valid & (level_of > 0), VERTICAL_MIX, 0.0).astype(jnp.float32)
    return valid, from_above, from_below


def put_coefficients(bufs, tile, to, rows, courant, viscosity, mix):
    a_buf, w_buf, v_buf = bufs
    a_buf[tile, pl.ds(to, rows), :] = 1.0 - courant - 4.0 * viscosity - mix
    w_buf[tile, pl.ds(to, rows), :] = courant + viscosity
    v_buf[tile, pl.ds(to, rows), :] = viscosity


def put_rim(u_buf, bufs, west, east, to, rows):
    _, place = rim_place(lane_ids())
    _, from_above, from_below = rim_mixes()
    zero = jnp.zeros((rows, CY), jnp.float32)
    start = 0
    found = []
    for width in (WIDE, MID, MID):
        value = jnp.where((place >= 0) & (place < width), rolled(east, -start), zero)
        found.append(
            jnp.where((place >= -width) & (place < 0), rolled(west, -start - width), value)
        )
        start += width
    u_buf[LEV, pl.ds(to, rows), :] = found[0]
    put_coefficients(bufs, LEV, to, rows, found[1], found[2], from_above + from_below)


def put_thin_rim(l_buf, west, east, block, to, rows):
    level_of, place = rim_place(lane_ids())
    value = jnp.zeros((rows, CY), jnp.float32)
    for level in range(LEV):
        at = GAP * level - (32 * block + THIN * level)
        mine = level_of == level
        value = jnp.where(mine & (place >= 0) & (place < THIN), rolled(east, at), value)
        value = jnp.where(mine & (place >= -THIN) & (place < 0), rolled(west, at - THIN), value)
    l_buf[LEV, pl.ds(to, rows), :] = value


def prepare(
    n_gx, n_gy, per_device,
    place_ref, info_ref, vel_ref, seed_ref, cou_ref, vis_ref, west_ref, east_ref,
    u_buf, l_buf, a_buf, w_buf, v_buf, d_buf, rows_buf, cols_buf,
):
    lane = lane_ids()
    level_of, place = rim_place(lane)
    level_one = level_of == 1
    valid, _, _ = rim_mixes()

    devices = info_ref.shape[0]
    my_gx = place_ref[0].astype(jnp.float32)
    my_gy = place_ref[1].astype(jnp.float32)
    col_of = jnp.where(place < 0, place, CY + place).astype(jnp.float32)
    row_lane = lax.broadcasted_iota(jnp.int32, (1, 3 * CY), 1).astype(jnp.float32)
    row_profiles, rim_profiles = [], []

    def near(delta, count):
        delta = jnp.where(delta >= count / 2, delta - count, delta)
        return jnp.where(delta < -count / 2, delta + count, delta)

    def profile(cells, first, width):
        at = cells - first
        centred = at - (FP - 1) / 2.0
        value = jnp.exp(-(centred * centred) / (2.0 * width * width))
        return jnp.where((at >= 0.0) & (at < float(FP)), value, 0.0)

    for k in range(per_device):
        info = info_ref[:, VALUES * k : VALUES * k + VALUES]
        row_first = near(info[:, 0:1] - my_gx, n_gx) * CX + info[:, 2:3]
        col_first = near(info[:, 1:2] - my_gy, n_gy) * CY + info[:, 3:4]
        scale = DRAG_SCALE * info[:, 4:5]
        width = info[:, 5:6]
        part = pl.ds(k * devices, devices)
        row_profiles.append(profile(row_lane - RIM, row_first, width) * scale)
        rows_buf[part, :] = profile(row_lane[:, :CX], row_first, width) * scale
        cols_buf[part, :] = profile(lane.astype(jnp.float32), col_first, width)
        rim_profiles.append(profile(col_of, col_first, width))
    along_rows = jnp.concatenate(row_profiles, axis=0)
    along_cols = jnp.concatenate([cols_buf[...], jnp.concatenate(rim_profiles, axis=0)], axis=1)
    drag = lax.dot_general(
        along_rows.T, along_cols, (((1,), (0,)), ((), ())),
        precision=lax.Precision.HIGHEST, preferred_element_type=jnp.float32,
    )
    tall = pl.ds(TOP - RIM, CX + 2 * RIM)
    gain = jnp.where(valid, jnp.where(level_one, 1.0, SIDE_GAIN), 0.0).astype(jnp.float32)
    d_buf[0, tall, :] = drag[: CX + 2 * RIM, :CY]
    d_buf[1, tall, :] = drag[: CX + 2 * RIM, :CY] * SIDE_GAIN
    d_buf[2, tall, :] = drag[: CX + 2 * RIM, CY:] * gain

    edge = jnp.zeros((TOP - RIM, CY), jnp.float32)
    for tile in range(LEV + 1):
        for buf in (a_buf, w_buf, v_buf, u_buf, l_buf):
            buf[tile, 0 : TOP - RIM, :] = edge
            buf[tile, TALL - TOP + RIM :, :] = edge
        l_buf[tile, TOP - RIM : TOP - THIN, :] = edge
        l_buf[tile, TOP + CX + THIN : TOP + CX + RIM, :] = edge
    inside = pl.ds(TOP, CX)
    bufs = (a_buf, w_buf, v_buf)
    for level in range(LEV):
        u_buf[level, inside, :] = vel_ref[level]
        l_buf[level, inside, :] = seed_ref[level]
        put_coefficients(bufs, level, TOP, CX, cou_ref[level], vis_ref[level], level_mix(level))
    put_rim(u_buf, bufs, west_ref[0:CX, :], east_ref[0:CX, :], TOP, CX)
    for block in range(4):
        at = pl.ds(CX, 64)
        put_thin_rim(l_buf, west_ref[at, :], east_ref[at, :], block, TOP + 64 * block, 64)


def window(
    per_device,
    u_even_in, l_even_in, a_in, w_in, v_in, d_buf, rows_buf, cols_buf, low_ref, high_ref,
    start_ref, grads_ref, u_even, l_even, a_buf, w_buf, v_buf,
    u_odd, l_odd, g_buf, f_buf, s_buf,
):
    u_buf, l_buf = (u_even, u_odd), (l_even, l_odd)
    bufs = (a_buf, w_buf, v_buf)
    lane = lane_ids()
    level_of, place = rim_place(lane)
    west_lane, east_lane = place == -1, place == 0
    level_one, level_two = level_of == 1, level_of == 2
    _, from_above, from_below = rim_mixes()
    first_lane, last_lane = lane == 0, lane == CY - 1
    devices = grads_ref.shape[0]

    edge = jnp.zeros((TOP - RIM, CY), jnp.float32)
    for tile in range(LEV + 1):
        for buf in (u_odd, l_odd):
            buf[tile, 0 : TOP - RIM, :] = edge
            buf[tile, TALL - TOP + RIM :, :] = edge
        l_odd[tile, TOP - RIM : TOP - THIN, :] = edge
        l_odd[tile, TOP + CX + THIN : TOP + CX + RIM, :] = edge
    for ref, to, thin_to, block in (
        (low_ref, TOP - RIM, TOP - THIN, 3),
        (high_ref, TOP + CX, TOP + CX, 0),
    ):
        for level in range(LEV):
            u_even[level, to : to + RIM, :] = ref[RIM * level : RIM * level + RIM, :]
            courant = ref[RIM * (LEV + level) : RIM * (LEV + level) + RIM, :]
            viscosity = ref[RIM * (2 * LEV + level) : RIM * (2 * LEV + level) + RIM, :]
            put_coefficients(bufs, level, to, RIM, courant, viscosity, level_mix(level))
            at = 3 * LEV * RIM + THIN * level
            l_even[level, thin_to : thin_to + THIN, :] = ref[at : at + THIN, :]
        at = 3 * LEV * RIM + LEV * THIN
        put_rim(u_even, bufs, ref[at : at + RIM, :], ref[at + RIM : at + 2 * RIM, :], to, RIM)
        at += 2 * RIM
        west, east = ref[at : at + THIN, :], ref[at + THIN : at + 2 * THIN, :]
        put_thin_rim(l_even, west, east, block, thin_to, THIN)

    def borders(tiles):
        packed = tiles[LEV]
        across = [rolled(packed, -GAP * level) for level in range(LEV)]
        other = jnp.where(level_one, rolled(tiles[1], GAP), tiles[0])
        across.append(jnp.where(level_two, rolled(tiles[2], 2 * GAP), other))
        return across

    def sideways(tiles, across, with_rim=True):
        sums = []
        for tile in range(LEV + 1 if with_rim else LEV):
            low, high = (west_lane, east_lane) if tile == LEV else (last_lane, first_lane)
            left = rolled(jnp.where(low, across[tile], tiles[tile]), 1)
            right = rolled(jnp.where(high, across[tile], tiles[tile]), -1)
            sums.append(left + right)
        return sums

    def upright(core):
        middle = VERTICAL_MIX * core[1]
        return [middle, VERTICAL_MIX * (core[0] + core[2]), middle]

    def rim_upright(packed):
        return from_above * rolled(packed, -GAP) + from_below * rolled(packed, GAP)

    def drag_of(tile, at):
        return d_buf[(1, 0, 1, 2)[tile], at, :]

    def drag_terms(state, drag_here):
        square = state * state + 1.0
        root = lax.rsqrt(square)
        weak = drag_here * root
        return square, root, weak, weak * square

    def staged(first, count, stages):
        chunks = [(first + at, min(CHUNK, count - at)) for at in range(0, count, CHUNK)]
        held = [None] * len(chunks)
        delay = (len(stages) - 1) * AHEAD
        for tick in range(len(chunks) + delay):
            for index, stage in enumerate(stages):
                at = tick - index * AHEAD
                if 0 <= at < len(chunks):
                    held[at] = stage(pl.ds(*chunks[at]), chunks[at], held[at])

    for step in range(STEPS - 1):
        rows_beyond = RIM if STEPS + 5 - step > 8 else 8
        now, later = step % 2, (step + 1) % 2

        def exchange(at, chunk, _, now=now):
            return borders([u_buf[now][tile, at, :] for tile in range(LEV + 1)])

        def shift(at, chunk, other, now=now):
            state = [u_buf[now][tile, at, :] for tile in range(LEV + 1)]
            return sideways(state, other), rim_upright(state[LEV])

        def advance(at, chunk, shifted, step=step, now=now, later=later):
            first, rows = chunk
            sides, mixed_rim = shifted
            state = [u_buf[now][tile, at, :] for tile in range(LEV + 1)]
            mixed = upright(state) + [mixed_rim]
            for tile in range(LEV + 1):
                upwind = u_buf[now][tile, pl.ds(first - 1, rows), :]
                downwind = u_buf[now][tile, pl.ds(first + 1, rows), :]
                square, root, weak, strong = drag_terms(state[tile], drag_of(tile, at))
                centre = a_buf[tile, at, :] - strong
                u_buf[later][tile, at, :] = (
                    centre * state[tile]
                    + w_buf[tile, at, :] * upwind
                    + v_buf[tile, at, :] * (downwind + sides[tile])
                    + mixed[tile]
                )
                g_buf[step, tile, at, :] = centre - strong + weak
                if tile < LEV:
                    f_buf[step, tile, at, :] = state[tile] * (square * root)

        staged(TOP - rows_beyond, CX + 2 * rows_beyond, (exchange, shift, advance))

    last = STEPS - 1

    def slopes(first, rows):
        at = pl.ds(first, rows)
        for tile in range(LEV + 1):
            state = u_buf[last % 2][tile, at, :]
            square, root, weak, strong = drag_terms(state, drag_of(tile, at))
            g_buf[last, tile, at, :] = a_buf[tile, at, :] - 2.0 * strong + weak
            if tile < LEV:
                f_buf[last, tile, at, :] = state * (square * root)

    for_rows(TOP - 8, CX + 16, CX + 16, slopes)

    zero = jnp.zeros((CX + 16, CY), jnp.float32)
    for part in range(2):
        s_buf[part, TOP - 8 : TOP + CX + 8, :] = zero
    for step in reversed(range(STEPS)):
        rows_beyond = 8 if step else 0
        now, later = (last - step) % 2, (last - step + 1) % 2

        def fluxes(at, now=now):
            adjoint = [l_buf[now][tile, at, :] for tile in range(LEV + 1)]
            return adjoint, [v_buf[tile, at, :] * adjoint[tile] for tile in range(LEV + 1)]

        def exchange(at, chunk, _, fluxes=fluxes):
            return borders(fluxes(at)[1])

        def shift(at, chunk, other, fluxes=fluxes, step=step):
            adjoint, flux = fluxes(at)
            return sideways(flux, other, bool(step)), rim_upright(adjoint[LEV]) if step else None

        def retreat(at, chunk, shifted, step=step, now=now, later=later):
            first, rows = chunk
            sides, mixed_rim = shifted
            before, after = pl.ds(first - 1, rows), pl.ds(first + 1, rows)
            adjoint = [l_buf[now][tile, at, :] for tile in range(LEV + 1)]
            mixed = upright(adjoint) + [mixed_rim]
            for tile in range(LEV + 1 if step else LEV):
                value = (
                    g_buf[step, tile, at, :] * adjoint[tile]
                    + w_buf[tile, after, :] * l_buf[now][tile, after, :]
                    + v_buf[tile, before, :] * l_buf[now][tile, before, :]
                    + sides[tile]
                    + mixed[tile]
                )
                if step:
                    l_buf[later][tile, at, :] = value
                else:
                    start_ref[tile, pl.ds(first - TOP, rows), :] = value
            s_buf[0, at, :] += f_buf[step, 1, at, :] * adjoint[1]
            s_buf[1, at, :] += (
                f_buf[step, 0, at, :] * adjoint[0] + f_buf[step, 2, at, :] * adjoint[2]
            )

        staged(TOP - rows_beyond, CX + 2 * rows_beyond, (exchange, shift, retreat))

    inside = pl.ds(TOP, CX)
    sensitivity = s_buf[0, inside, :] + SIDE_GAIN * s_buf[1, inside, :]
    across = lax.dot_general(
        rows_buf[...], sensitivity, (((1,), (0,)), ((), ())),
        precision=lax.Precision.HIGHEST, preferred_element_type=jnp.float32,
    )
    sums = -jnp.sum(across * cols_buf[...], axis=1, keepdims=True)
    grads = jnp.zeros((devices, CY), jnp.float32)
    for k in range(per_device):
        mine = spread_lanes(sums[k * devices : (k + 1) * devices, :], devices)
        grads = jnp.where(lane == k, mine, grads)
    grads_ref[...] = grads


def shards(
    velocity, adjoint_seed, courant, viscosity, turbine_tile, turbine_offset, thrust, disk_width
):
    n_gx, n_gy = lax.axis_size("gx"), lax.axis_size("gy")
    devices = n_gx * n_gy
    per_device = thrust.shape[0]
    f32 = jnp.float32
    smem = pl.BlockSpec(memory_space=pltpu.SMEM)
    vmem = pl.BlockSpec(memory_space=pltpu.VMEM)

    def ring(axis, by):
        count = lax.axis_size(axis)
        return [(i, (i + by) % count) for i in range(count)]

    side_up, side_down, info = pl.pallas_call(
        functools.partial(pack_sides, n_gy),
        name="pack_sides",
        out_shape=(
            jax.ShapeDtypeStruct((SIDE_ROWS, CY), f32),
            jax.ShapeDtypeStruct((SIDE_ROWS, CY), f32),
            jax.ShapeDtypeStruct((devices, CY), f32),
        ),
        in_specs=[pl.BlockSpec(memory_space=pl.ANY)] * 8,
        out_specs=(vmem,) * 3,
        scratch_shapes=[
            pltpu.SMEM((per_device,), jnp.int32),
            pltpu.SMEM((2, per_device), jnp.int32),
            pltpu.SMEM((per_device,), f32),
            pltpu.SMEM((per_device,), f32),
            *[pltpu.VMEM((LEV, CX, CY), f32)] * 4,
            pltpu.SemaphoreType.DMA((8,)),
        ],
    )(turbine_tile.reshape(per_device), turbine_offset.T, thrust, disk_width, velocity, adjoint_seed, courant, viscosity)
    west = lax.ppermute(side_up, "gy", ring("gy", 1))
    east = lax.ppermute(side_down, "gy", ring("gy", -1))
    info = lax.all_to_all(info, ("gx", "gy"), 0, 0, tiled=True)
    end_up, end_down = pl.pallas_call(
        pack_ends,
        name="pack_ends",
        out_shape=(jax.ShapeDtypeStruct((END_ROWS, CY), f32),) * 2,
        in_specs=[vmem] * 6,
        out_specs=(vmem,) * 2,
        compiler_params=SMALL,
    )(west, east, velocity, adjoint_seed, courant, viscosity)
    low = lax.ppermute(end_up, "gx", ring("gx", 1))
    high = lax.ppermute(end_down, "gx", ring("gx", -1))
    place = jnp.stack([lax.axis_index("gx"), lax.axis_index("gy")]).astype(jnp.int32)
    turbines = devices * per_device
    field = jax.ShapeDtypeStruct((LEV + 1, TALL, CY), f32)
    fields = pl.pallas_call(
        functools.partial(prepare, n_gx, n_gy, per_device),
        name="prepare",
        out_shape=(
            *[field] * 5,
            jax.ShapeDtypeStruct((3, TALL, CY), f32),
            jax.ShapeDtypeStruct((turbines, CX), f32),
            jax.ShapeDtypeStruct((turbines, CY), f32),
        ),
        in_specs=[smem] + [vmem] * 7,
        out_specs=(vmem,) * 8,
        compiler_params=SMALL,
        cost_estimate=pl.CostEstimate(flops=40000000, bytes_accessed=8000000, transcendentals=0),
    )(place, info, velocity, adjoint_seed, courant, viscosity, west, east)
    adjoint_start, grads, *_ = pl.pallas_call(
        functools.partial(window, per_device),
        name="window",
        out_shape=(
            jax.ShapeDtypeStruct((LEV, CX, CY), f32),
            jax.ShapeDtypeStruct((devices, CY), f32),
            *[field] * 5,
        ),
        in_specs=[vmem] * 10,
        out_specs=(vmem,) * 7,
        input_output_aliases={index: index + 2 for index in range(5)},
        scratch_shapes=[
            pltpu.VMEM((LEV + 1, TALL, CY), f32),
            pltpu.VMEM((LEV + 1, TALL, CY), f32),
            pltpu.VMEM((STEPS, LEV + 1, TALL, CY), f32),
            pltpu.VMEM((STEPS, LEV, TALL, CY), f32),
            pltpu.VMEM((2, TALL, CY), f32),
        ],
        compiler_params=pltpu.CompilerParams(vmem_limit_bytes=24 * 1024 * 1024),
    )(*fields, low, high)
    grads = lax.all_to_all(grads, ("gx", "gy"), 0, 0, tiled=True)
    return adjoint_start, jnp.sum(grads, axis=0)[:per_device]


def solution(mesh):
    tiled = P(None, "gx", "gy")
    spread = P(("gx", "gy"))
    matrix = P(("gx", "gy"), None)
    return jax.shard_map(
        shards,
        mesh=mesh,
        in_specs=(tiled, tiled, tiled, tiled, matrix, matrix, spread, spread),
        out_specs=(tiled, spread),
        check_vma=False,
    )
```

```python
import functools
import math

import jax
import jax.numpy as jnp
from jax import lax
from jax.experimental import pallas as pl
from jax.experimental.pallas import tpu as pltpu
from jax.sharding import PartitionSpec as P

STEPS = 8
FP = 64
VERTICAL_MIX = 0.05
DRAG_SCALE = 0.01
SIDE_GAIN = math.exp(-0.5)

LEV, CX, CY = 3, 256, 128
WIDE = 14
MID = 13
THIN = 8
GAP = 42
CENTRE = (CY - GAP, 0, GAP)
RIM = 16
TOP = 24
TALL = CX + 2 * TOP
SIDE_ROWS = CX + 64
END_ROWS = 3 * LEV * RIM + LEV * THIN + 2 * RIM + 2 * THIN
VALUES = 6
CHUNK = 32
AHEAD = 2
SMALL = pltpu.CompilerParams(vmem_limit_bytes=8 * 1024 * 1024)


def lane_ids():
    return lax.broadcasted_iota(jnp.int32, (1, CY), 1)


def spread_lanes(value, rows):
    return jnp.broadcast_to(value, (rows, CY))


def rolled(value, shift):
    shift = shift % CY
    return value if shift == 0 else pltpu.roll(value, shift, 1)


def rim_place(lane):
    level = jnp.where((lane >= GAP // 2) & (lane < CY // 2), 2, 1)
    level = jnp.where((lane >= CY // 2) & (lane < CY - GAP // 2), 0, level)
    place = lane - jnp.where(level == 2, GAP, jnp.where(level == 0, CY - GAP, 0))
    place = jnp.where(lane >= CY - GAP // 2, lane - CY, place)
    return level, place


def for_rows(first, count, chunk, body):
    full = count // chunk
    if full == 1:
        body(first, chunk)
    elif full > 1:

        def one(index, carry):
            body(pl.multiple_of(first + index * chunk, 8), chunk)
            return carry

        lax.fori_loop(0, full, one, 0)
    if count > full * chunk:
        body(first + full * chunk, count - full * chunk)


def pack_sides(
    n_gy, tile_hbm, offset_hbm, thrust_hbm, width_hbm, vel_hbm, seed_hbm, cou_hbm, vis_hbm,
    up_ref, down_ref, info_ref,
    tile_ref, offset_ref, thrust_ref, width_ref, vel_ref, seed_ref, cou_ref, vis_ref, arrived,
):
    copies = [
        pltpu.make_async_copy(source, target, arrived.at[index])
        for index, (source, target) in enumerate(
            (
                (seed_hbm, seed_ref), (vel_hbm, vel_ref), (cou_hbm, cou_ref), (vis_hbm, vis_ref),
                (tile_hbm, tile_ref), (offset_hbm, offset_ref), (thrust_hbm, thrust_ref),
                (width_hbm, width_ref),
            )
        )
    ]
    for copy in copies:
        copy.start()
    lane = lane_ids()
    level_of, _ = rim_place(lane)
    for copy in copies[4:]:
        copy.wait()
    whole = jnp.zeros((1, CY), jnp.int32)
    real = jnp.zeros((1, CY), jnp.float32)
    for k in range(thrust_ref.shape[0]):
        tile = tile_ref[k]
        for spot, value in enumerate(
            (tile // n_gy, tile % n_gy, offset_ref[0, k], offset_ref[1, k])
        ):
            whole = jnp.where(lane == VALUES * k + spot, value, whole)
        real = jnp.where(lane == VALUES * k + 4, thrust_ref[k], real)
        real = jnp.where(lane == VALUES * k + 5, width_ref[k], real)
    info_ref[...] = jnp.broadcast_to(whole.astype(jnp.float32) + real, info_ref.shape)

    copies[0].wait()
    for out_ref, low in ((up_ref, False), (down_ref, True)):
        total = jnp.zeros((64, CY), jnp.float32)
        for block in range(4):
            for level in range(LEV):
                to = 32 * block + THIN * level
                moved = rolled(
                    seed_ref[level, 64 * block : 64 * block + 64, :],
                    to - (0 if low else CY - THIN),
                )
                total = jnp.where((lane >= to) & (lane < to + THIN), moved, total)
        out_ref[CX:SIDE_ROWS, :] = total

    def around(ref):
        value = jnp.where(level_of == 0, rolled(ref[0], -GAP), ref[1])
        return jnp.where(level_of == 2, rolled(ref[2], GAP), value)

    up = down = None
    for index, (ref, width) in enumerate(((vel_ref, WIDE), (cou_ref, MID), (vis_ref, MID))):
        copies[1 + index].wait()
        both = around(ref)
        start = (0, WIDE, WIDE + MID)[index]
        if index == 0:
            up, down = rolled(both, width), both
        else:
            mine = in_share(lane, start, width)
            up = jnp.where(mine, rolled(both, start + width), up)
            down = jnp.where(mine, rolled(both, start), down)
    up_ref[0:CX, :] = up
    down_ref[0:CX, :] = down


def in_share(lane, start, width):
    inside = jnp.zeros(lane.shape, jnp.bool_)
    for level in range(LEV):
        first = CENTRE[level] + start
        inside = inside | ((lane >= first) & (lane < first + width))
    return inside


def pack_ends(west_ref, east_ref, vel_ref, seed_ref, cou_ref, vis_ref, up_ref, down_ref):
    for out_ref, low in ((up_ref, False), (down_ref, True)):
        at = 0
        first = 0 if low else CX - RIM
        for ref in (vel_ref, cou_ref, vis_ref):
            for level in range(LEV):
                out_ref[at : at + RIM, :] = ref[level, first : first + RIM, :]
                at += RIM
        thin_first = 0 if low else CX - THIN
        for level in range(LEV):
            out_ref[at : at + THIN, :] = seed_ref[level, thin_first : thin_first + THIN, :]
            at += THIN
        for ref in (west_ref, east_ref):
            out_ref[at : at + RIM, :] = ref[first : first + RIM, :]
            at += RIM
        side_first = CX if low else SIDE_ROWS - THIN
        for ref in (west_ref, east_ref):
            out_ref[at : at + THIN, :] = ref[side_first : side_first + THIN, :]
            at += THIN


def level_mix(level):
    return VERTICAL_MIX * (2 if level == 1 else 1)


def rim_mixes():
    level_of, place = rim_place(lane_ids())
    valid = (place >= -WIDE) & (place < WIDE)
    upper = jnp.where(valid & (level_of != 2), VERTICAL_MIX, 0.0).astype(jnp.float32)
    lower = jnp.where(valid & (level_of != 0), VERTICAL_MIX, 0.0).astype(jnp.float32)
    return valid, upper, lower


def put_coefficients(bufs, tile, to, rows, courant, viscosity, mix):
    a_buf, w_buf, v_buf = bufs
    a_buf[tile, pl.ds(to, rows), :] = 1.0 - courant - 4.0 * viscosity - mix
    w_buf[tile, pl.ds(to, rows), :] = courant + viscosity
    v_buf[tile, pl.ds(to, rows), :] = viscosity


def put_rim(u_buf, bufs, west, east, to, rows):
    _, place = rim_place(lane_ids())
    _, upper, lower = rim_mixes()
    zero = jnp.zeros((rows, CY), jnp.float32)
    start = 0
    found = []
    for width in (WIDE, MID, MID):
        value = jnp.where((place >= 0) & (place < width), rolled(east, -start), zero)
        found.append(
            jnp.where((place >= -width) & (place < 0), rolled(west, -start - width), value)
        )
        start += width
    u_buf[LEV, pl.ds(to, rows), :] = found[0]
    put_coefficients(bufs, LEV, to, rows, found[1], found[2], upper + lower)


def put_thin_rim(l_buf, west, east, block, to, rows):
    level_of, place = rim_place(lane_ids())
    value = jnp.zeros((rows, CY), jnp.float32)
    for level in range(LEV):
        at = CENTRE[level] - (32 * block + THIN * level)
        mine = level_of == level
        value = jnp.where(mine & (place >= 0) & (place < THIN), rolled(east, at), value)
        value = jnp.where(mine & (place >= -THIN) & (place < 0), rolled(west, at - THIN), value)
    l_buf[LEV, pl.ds(to, rows), :] = value


def prepare(
    n_gx, n_gy, per_device,
    place_ref, info_ref, vel_ref, seed_ref, cou_ref, vis_ref, west_ref, east_ref,
    u_buf, l_buf, a_buf, w_buf, v_buf, d_buf, rows_buf, cols_buf,
):
    lane = lane_ids()
    level_of, place = rim_place(lane)
    level_one = level_of == 1
    valid, _, _ = rim_mixes()

    devices = info_ref.shape[0]
    my_gx = place_ref[0].astype(jnp.float32)
    my_gy = place_ref[1].astype(jnp.float32)
    col_of = jnp.where(place < 0, place, CY + place).astype(jnp.float32)
    row_lane = lax.broadcasted_iota(jnp.int32, (1, 3 * CY), 1).astype(jnp.float32)
    row_profiles, rim_profiles = [], []

    def near(delta, count):
        delta = jnp.where(delta >= count / 2, delta - count, delta)
        return jnp.where(delta < -count / 2, delta + count, delta)

    def profile(cells, first, width):
        at = cells - first
        centred = at - (FP - 1) / 2.0
        value = jnp.exp(-(centred * centred) / (2.0 * width * width))
        return jnp.where((at >= 0.0) & (at < float(FP)), value, 0.0)

    for k in range(per_device):
        info = info_ref[:, VALUES * k : VALUES * k + VALUES]
        row_first = near(info[:, 0:1] - my_gx, n_gx) * CX + info[:, 2:3]
        col_first = near(info[:, 1:2] - my_gy, n_gy) * CY + info[:, 3:4]
        scale = DRAG_SCALE * info[:, 4:5]
        width = info[:, 5:6]
        part = pl.ds(k * devices, devices)
        row_profiles.append(profile(row_lane - RIM, row_first, width) * scale)
        rows_buf[part, :] = profile(row_lane[:, :CX], row_first, width) * scale
        cols_buf[part, :] = profile(lane.astype(jnp.float32), col_first, width)
        rim_profiles.append(profile(col_of, col_first, width))
    along_rows = jnp.concatenate(row_profiles, axis=0)
    along_cols = jnp.concatenate([cols_buf[...], jnp.concatenate(rim_profiles, axis=0)], axis=1)
    drag = lax.dot_general(
        along_rows.T, along_cols, (((1,), (0,)), ((), ())),
        precision=lax.Precision.HIGHEST, preferred_element_type=jnp.float32,
    )
    tall = pl.ds(TOP - RIM, CX + 2 * RIM)
    gain = jnp.where(valid, jnp.where(level_one, 1.0, SIDE_GAIN), 0.0).astype(jnp.float32)
    d_buf[0, tall, :] = drag[: CX + 2 * RIM, :CY]
    d_buf[1, tall, :] = drag[: CX + 2 * RIM, :CY] * SIDE_GAIN
    d_buf[2, tall, :] = drag[: CX + 2 * RIM, CY:] * gain

    edge = jnp.zeros((TOP - RIM, CY), jnp.float32)
    for tile in range(LEV + 1):
        for buf in (a_buf, w_buf, v_buf, u_buf, l_buf):
            buf[tile, 0 : TOP - RIM, :] = edge
            buf[tile, TALL - TOP + RIM :, :] = edge
        l_buf[tile, TOP - RIM : TOP - THIN, :] = edge
        l_buf[tile, TOP + CX + THIN : TOP + CX + RIM, :] = edge
    inside = pl.ds(TOP, CX)
    bufs = (a_buf, w_buf, v_buf)
    for level in range(LEV):
        u_buf[level, inside, :] = vel_ref[level]
        l_buf[level, inside, :] = seed_ref[level]
        put_coefficients(bufs, level, TOP, CX, cou_ref[level], vis_ref[level], level_mix(level))
    put_rim(u_buf, bufs, west_ref[0:CX, :], east_ref[0:CX, :], TOP, CX)
    for block in range(4):
        at = pl.ds(CX, 64)
        put_thin_rim(l_buf, west_ref[at, :], east_ref[at, :], block, TOP + 64 * block, 64)


def window(
    per_device,
    u_even_in, l_even_in, a_in, w_in, v_in, d_buf, rows_buf, cols_buf, low_ref, high_ref,
    start_ref, grads_ref, u_even, l_even, a_buf, w_buf, v_buf,
    u_odd, l_odd, g_buf, f_buf, s_buf, v_turned,
):
    u_buf, l_buf = (u_even, u_odd), (l_even, l_odd)
    bufs = (a_buf, w_buf, v_buf)
    lane = lane_ids()
    level_of, place = rim_place(lane)
    west_lane, east_lane = place == -1, place == 0
    level_zero, level_two = level_of == 0, level_of == 2
    _, upper, lower = rim_mixes()
    first_lane, last_lane = lane == 0, lane == CY - 1
    devices = grads_ref.shape[0]

    edge = jnp.zeros((TOP - RIM, CY), jnp.float32)
    for tile in range(LEV + 1):
        for buf in (u_odd, l_odd):
            buf[tile, 0 : TOP - RIM, :] = edge
            buf[tile, TALL - TOP + RIM :, :] = edge
        l_odd[tile, TOP - RIM : TOP - THIN, :] = edge
        l_odd[tile, TOP + CX + THIN : TOP + CX + RIM, :] = edge
    for ref, to, thin_to, block in (
        (low_ref, TOP - RIM, TOP - THIN, 3),
        (high_ref, TOP + CX, TOP + CX, 0),
    ):
        for level in range(LEV):
            u_even[level, to : to + RIM, :] = ref[RIM * level : RIM * level + RIM, :]
            courant = ref[RIM * (LEV + level) : RIM * (LEV + level) + RIM, :]
            viscosity = ref[RIM * (2 * LEV + level) : RIM * (2 * LEV + level) + RIM, :]
            put_coefficients(bufs, level, to, RIM, courant, viscosity, level_mix(level))
            at = 3 * LEV * RIM + THIN * level
            l_even[level, thin_to : thin_to + THIN, :] = ref[at : at + THIN, :]
        at = 3 * LEV * RIM + LEV * THIN
        put_rim(u_even, bufs, ref[at : at + RIM, :], ref[at + RIM : at + 2 * RIM, :], to, RIM)
        at += 2 * RIM
        west, east = ref[at : at + THIN, :], ref[at + THIN : at + 2 * THIN, :]
        put_thin_rim(l_even, west, east, block, thin_to, THIN)

    def beyond(packed):
        return rolled(packed, GAP), rolled(packed, -GAP)

    def outward(tiles):
        other = jnp.where(level_zero, rolled(tiles[0], -GAP), tiles[1])
        return jnp.where(level_two, rolled(tiles[2], GAP), other)

    def sideways(tiles, across, with_rim=True):
        sums = []
        for tile in range(LEV + 1 if with_rim else LEV):
            low, high = (west_lane, east_lane) if tile == LEV else (last_lane, first_lane)
            left = rolled(jnp.where(low, across[tile], tiles[tile]), 1)
            right = rolled(jnp.where(high, across[tile], tiles[tile]), -1)
            sums.append(left + right)
        return sums

    def upright(core):
        middle = VERTICAL_MIX * core[1]
        return [middle, VERTICAL_MIX * (core[0] + core[2]), middle]

    def rim_upright(plus, minus):
        return upper * minus + lower * plus

    for index, turned in enumerate(beyond(v_buf[LEV, TOP - 8 : TOP + CX + 8, :])):
        v_turned[index, TOP - 8 : TOP + CX + 8, :] = turned

    def drag_of(tile, at):
        return d_buf[(1, 0, 1, 2)[tile], at, :]

    def drag_terms(state, drag_here):
        square = state * state + 1.0
        root = lax.rsqrt(square)
        weak = drag_here * root
        return square, root, weak, weak * square

    def staged(first, count, stages):
        chunks = [(first + at, min(CHUNK, count - at)) for at in range(0, count, CHUNK)]
        held = [None] * len(chunks)
        delay = (len(stages) - 1) * AHEAD
        for tick in range(len(chunks) + delay):
            for index, stage in enumerate(stages):
                at = tick - index * AHEAD
                if 0 <= at < len(chunks):
                    held[at] = stage(pl.ds(*chunks[at]), chunks[at], held[at])

    for step in range(STEPS - 1):
        rows_beyond = RIM if STEPS + 5 - step > 8 else 8
        now, later = step % 2, (step + 1) % 2

        def exchange(at, chunk, _, now=now):
            state = [u_buf[now][tile, at, :] for tile in range(LEV + 1)]
            return *beyond(state[LEV]), outward(state)

        def shift(at, chunk, held, now=now):
            plus, minus, other = held
            state = [u_buf[now][tile, at, :] for tile in range(LEV + 1)]
            return sideways(state, (plus, state[LEV], minus, other)), rim_upright(plus, minus)

        def advance(at, chunk, shifted, step=step, now=now, later=later):
            first, rows = chunk
            sides, mixed_rim = shifted
            state = [u_buf[now][tile, at, :] for tile in range(LEV + 1)]
            mixed = upright(state) + [mixed_rim]
            for tile in range(LEV + 1):
                upwind = u_buf[now][tile, pl.ds(first - 1, rows), :]
                downwind = u_buf[now][tile, pl.ds(first + 1, rows), :]
                square, root, weak, strong = drag_terms(state[tile], drag_of(tile, at))
                centre = a_buf[tile, at, :] - strong
                u_buf[later][tile, at, :] = (
                    centre * state[tile]
                    + w_buf[tile, at, :] * upwind
                    + v_buf[tile, at, :] * (downwind + sides[tile])
                    + mixed[tile]
                )
                g_buf[step, tile, at, :] = centre - strong + weak
                if tile < LEV:
                    f_buf[step, tile, at, :] = state[tile] * (square * root)

        staged(TOP - rows_beyond, CX + 2 * rows_beyond, (exchange, shift, advance))

    last = STEPS - 1

    def slopes(first, rows):
        at = pl.ds(first, rows)
        for tile in range(LEV + 1):
            state = u_buf[last % 2][tile, at, :]
            square, root, weak, strong = drag_terms(state, drag_of(tile, at))
            g_buf[last, tile, at, :] = a_buf[tile, at, :] - 2.0 * strong + weak
            if tile < LEV:
                f_buf[last, tile, at, :] = state * (square * root)

    for_rows(TOP - 8, CX + 16, CX + 16, slopes)

    zero = jnp.zeros((CX + 16, CY), jnp.float32)
    for part in range(2):
        s_buf[part, TOP - 8 : TOP + CX + 8, :] = zero
    for step in reversed(range(STEPS)):
        rows_beyond = 8 if step else 0
        now, later = (last - step) % 2, (last - step + 1) % 2

        def fluxes(at, now=now):
            adjoint = [l_buf[now][tile, at, :] for tile in range(LEV + 1)]
            return adjoint, [v_buf[tile, at, :] * adjoint[tile] for tile in range(LEV + 1)]

        def exchange(at, chunk, _, fluxes=fluxes):
            adjoint, flux = fluxes(at)
            return *beyond(adjoint[LEV]), outward(flux)

        def shift(at, chunk, held, fluxes=fluxes, step=step):
            plus, minus, other = held
            flux = fluxes(at)[1]
            across = plus * v_turned[0, at, :], flux[LEV], minus * v_turned[1, at, :], other
            return sideways(flux, across, bool(step)), rim_upright(plus, minus) if step else None

        def retreat(at, chunk, shifted, step=step, now=now, later=later):
            first, rows = chunk
            sides, mixed_rim = shifted
            before, after = pl.ds(first - 1, rows), pl.ds(first + 1, rows)
            adjoint = [l_buf[now][tile, at, :] for tile in range(LEV + 1)]
            mixed = upright(adjoint) + [mixed_rim]
            for tile in range(LEV + 1 if step else LEV):
                value = (
                    g_buf[step, tile, at, :] * adjoint[tile]
                    + w_buf[tile, after, :] * l_buf[now][tile, after, :]
                    + v_buf[tile, before, :] * l_buf[now][tile, before, :]
                    + sides[tile]
                    + mixed[tile]
                )
                if step:
                    l_buf[later][tile, at, :] = value
                else:
                    start_ref[tile, pl.ds(first - TOP, rows), :] = value
            s_buf[0, at, :] += f_buf[step, 1, at, :] * adjoint[1]
            s_buf[1, at, :] += (
                f_buf[step, 0, at, :] * adjoint[0] + f_buf[step, 2, at, :] * adjoint[2]
            )

        staged(TOP - rows_beyond, CX + 2 * rows_beyond, (exchange, shift, retreat))

    inside = pl.ds(TOP, CX)
    sensitivity = s_buf[0, inside, :] + SIDE_GAIN * s_buf[1, inside, :]
    across = lax.dot_general(
        rows_buf[...], sensitivity, (((1,), (0,)), ((), ())),
        precision=lax.Precision.HIGHEST, preferred_element_type=jnp.float32,
    )
    sums = -jnp.sum(across * cols_buf[...], axis=1, keepdims=True)
    grads = jnp.zeros((devices, CY), jnp.float32)
    for k in range(per_device):
        mine = spread_lanes(sums[k * devices : (k + 1) * devices, :], devices)
        grads = jnp.where(lane == k, mine, grads)
    grads_ref[...] = grads


def shards(
    velocity, adjoint_seed, courant, viscosity, turbine_tile, turbine_offset, thrust, disk_width
):
    n_gx, n_gy = lax.axis_size("gx"), lax.axis_size("gy")
    devices = n_gx * n_gy
    per_device = thrust.shape[0]
    f32 = jnp.float32
    smem = pl.BlockSpec(memory_space=pltpu.SMEM)
    vmem = pl.BlockSpec(memory_space=pltpu.VMEM)

    def ring(axis, by):
        count = lax.axis_size(axis)
        return [(i, (i + by) % count) for i in range(count)]

    side_up, side_down, info = pl.pallas_call(
        functools.partial(pack_sides, n_gy),
        name="pack_sides",
        out_shape=(
            jax.ShapeDtypeStruct((SIDE_ROWS, CY), f32),
            jax.ShapeDtypeStruct((SIDE_ROWS, CY), f32),
            jax.ShapeDtypeStruct((devices, CY), f32),
        ),
        in_specs=[pl.BlockSpec(memory_space=pl.ANY)] * 8,
        out_specs=(vmem,) * 3,
        scratch_shapes=[
            pltpu.SMEM((per_device,), jnp.int32),
            pltpu.SMEM((2, per_device), jnp.int32),
            pltpu.SMEM((per_device,), f32),
            pltpu.SMEM((per_device,), f32),
            *[pltpu.VMEM((LEV, CX, CY), f32)] * 4,
            pltpu.SemaphoreType.DMA((8,)),
        ],
    )(turbine_tile.reshape(per_device), turbine_offset.T, thrust, disk_width, velocity, adjoint_seed, courant, viscosity)
    west = lax.ppermute(side_up, "gy", ring("gy", 1))
    east = lax.ppermute(side_down, "gy", ring("gy", -1))
    info = lax.all_to_all(info, ("gx", "gy"), 0, 0, tiled=True)
    end_up, end_down = pl.pallas_call(
        pack_ends,
        name="pack_ends",
        out_shape=(jax.ShapeDtypeStruct((END_ROWS, CY), f32),) * 2,
        in_specs=[vmem] * 6,
        out_specs=(vmem,) * 2,
        compiler_params=SMALL,
    )(west, east, velocity, adjoint_seed, courant, viscosity)
    low = lax.ppermute(end_up, "gx", ring("gx", 1))
    high = lax.ppermute(end_down, "gx", ring("gx", -1))
    place = jnp.stack([lax.axis_index("gx"), lax.axis_index("gy")]).astype(jnp.int32)
    turbines = devices * per_device
    field = jax.ShapeDtypeStruct((LEV + 1, TALL, CY), f32)
    fields = pl.pallas_call(
        functools.partial(prepare, n_gx, n_gy, per_device),
        name="prepare",
        out_shape=(
            *[field] * 5,
            jax.ShapeDtypeStruct((3, TALL, CY), f32),
            jax.ShapeDtypeStruct((turbines, CX), f32),
            jax.ShapeDtypeStruct((turbines, CY), f32),
        ),
        in_specs=[smem] + [vmem] * 7,
        out_specs=(vmem,) * 8,
        compiler_params=SMALL,
        cost_estimate=pl.CostEstimate(flops=40000000, bytes_accessed=8000000, transcendentals=0),
    )(place, info, velocity, adjoint_seed, courant, viscosity, west, east)
    adjoint_start, grads, *_ = pl.pallas_call(
        functools.partial(window, per_device),
        name="window",
        out_shape=(
            jax.ShapeDtypeStruct((LEV, CX, CY), f32),
            jax.ShapeDtypeStruct((devices, CY), f32),
            *[field] * 5,
        ),
        in_specs=[vmem] * 10,
        out_specs=(vmem,) * 7,
        input_output_aliases={index: index + 2 for index in range(5)},
        scratch_shapes=[
            pltpu.VMEM((LEV + 1, TALL, CY), f32),
            pltpu.VMEM((LEV + 1, TALL, CY), f32),
            pltpu.VMEM((STEPS, LEV + 1, TALL, CY), f32),
            pltpu.VMEM((STEPS, LEV, TALL, CY), f32),
            pltpu.VMEM((2, TALL, CY), f32),
            pltpu.VMEM((2, TALL, CY), f32),
        ],
        compiler_params=pltpu.CompilerParams(vmem_limit_bytes=24 * 1024 * 1024),
    )(*fields, low, high)
    grads = lax.all_to_all(grads, ("gx", "gy"), 0, 0, tiled=True)
    return adjoint_start, jnp.sum(grads, axis=0)[:per_device]


def solution(mesh):
    tiled = P(None, "gx", "gy")
    spread = P(("gx", "gy"))
    matrix = P(("gx", "gy"), None)
    return jax.shard_map(
        shards,
        mesh=mesh,
        in_specs=(tiled, tiled, tiled, tiled, matrix, matrix, spread, spread),
        out_specs=(tiled, spread),
        check_vma=False,
    )
```

```python
import functools
import math

import jax
import jax.numpy as jnp
from jax import lax
from jax.experimental import pallas as pl
from jax.experimental.pallas import tpu as pltpu
from jax.sharding import PartitionSpec as P

STEPS = 8
FP = 64
VERTICAL_MIX = 0.05
DRAG_SCALE = 0.01
SIDE_GAIN = math.exp(-0.5)

LEV, CX, CY = 3, 256, 128
WIDE = 14
MID = 13
THIN = 8
GAP = 42
CENTRE = (CY - GAP, 0, GAP)
RIM = 16
TOP = 24
TALL = CX + 2 * TOP
SIDE_ROWS = CX + 64
END_ROWS = 3 * LEV * RIM + LEV * THIN + 2 * RIM + 2 * THIN
VALUES = 6
CHUNK = 32
AHEAD = 2
SMALL = pltpu.CompilerParams(vmem_limit_bytes=8 * 1024 * 1024)


def lane_ids():
    return lax.broadcasted_iota(jnp.int32, (1, CY), 1)


def spread_lanes(value, rows):
    return jnp.broadcast_to(value, (rows, CY))


def rolled(value, shift):
    shift = shift % CY
    return value if shift == 0 else pltpu.roll(value, shift, 1)


def rim_place(lane):
    level = jnp.where((lane >= GAP // 2) & (lane < CY // 2), 2, 1)
    level = jnp.where((lane >= CY // 2) & (lane < CY - GAP // 2), 0, level)
    place = lane - jnp.where(level == 2, GAP, jnp.where(level == 0, CY - GAP, 0))
    place = jnp.where(lane >= CY - GAP // 2, lane - CY, place)
    return level, place


def for_rows(first, count, chunk, body):
    full = count // chunk
    if full == 1:
        body(first, chunk)
    elif full > 1:

        def one(index, carry):
            body(pl.multiple_of(first + index * chunk, 8), chunk)
            return carry

        lax.fori_loop(0, full, one, 0)
    if count > full * chunk:
        body(first + full * chunk, count - full * chunk)


def is_odd(axis):
    return lax.axis_index(axis) % 2 == 1


def in_order(axis, first, second):
    odd = is_odd(axis)
    return jnp.where(odd, second, first), jnp.where(odd, first, second)


def pack_sides(
    n_gy, tile_hbm, offset_hbm, thrust_hbm, width_hbm, vel_hbm, seed_hbm, cou_hbm, vis_hbm,
    outer_ref, inner_ref, info_ref,
    tile_ref, offset_ref, thrust_ref, width_ref, vel_ref, seed_ref, cou_ref, vis_ref, arrived,
):
    copies = [
        pltpu.make_async_copy(source, target, arrived.at[index])
        for index, (source, target) in enumerate(
            (
                (seed_hbm, seed_ref), (vel_hbm, vel_ref), (cou_hbm, cou_ref), (vis_hbm, vis_ref),
                (tile_hbm, tile_ref), (offset_hbm, offset_ref), (thrust_hbm, thrust_ref),
                (width_hbm, width_ref),
            )
        )
    ]
    for copy in copies:
        copy.start()
    lane = lane_ids()
    level_of, _ = rim_place(lane)
    for copy in copies[4:]:
        copy.wait()
    whole = jnp.zeros((1, CY), jnp.int32)
    real = jnp.zeros((1, CY), jnp.float32)
    for k in range(thrust_ref.shape[0]):
        tile = tile_ref[k]
        for spot, value in enumerate(
            (tile // n_gy, tile % n_gy, offset_ref[0, k], offset_ref[1, k])
        ):
            whole = jnp.where(lane == VALUES * k + spot, value, whole)
        real = jnp.where(lane == VALUES * k + 4, thrust_ref[k], real)
        real = jnp.where(lane == VALUES * k + 5, width_ref[k], real)
    info_ref[...] = jnp.broadcast_to(whole.astype(jnp.float32) + real, info_ref.shape)

    copies[0].wait()
    thin = []
    for low in (True, False):
        total = jnp.zeros((64, CY), jnp.float32)
        for block in range(4):
            for level in range(LEV):
                to = 32 * block + THIN * level
                moved = rolled(
                    seed_ref[level, 64 * block : 64 * block + 64, :],
                    to - (0 if low else CY - THIN),
                )
                total = jnp.where((lane >= to) & (lane < to + THIN), moved, total)
        thin.append(total)
    outer_ref[CX:SIDE_ROWS, :], inner_ref[CX:SIDE_ROWS, :] = in_order("gy", *thin)

    def around(ref):
        value = jnp.where(level_of == 0, rolled(ref[0], -GAP), ref[1])
        return jnp.where(level_of == 2, rolled(ref[2], GAP), value)

    up = down = None
    for index, (ref, width) in enumerate(((vel_ref, WIDE), (cou_ref, MID), (vis_ref, MID))):
        copies[1 + index].wait()
        both = around(ref)
        start = (0, WIDE, WIDE + MID)[index]
        if index == 0:
            up, down = rolled(both, width), both
        else:
            mine = in_share(lane, start, width)
            up = jnp.where(mine, rolled(both, start + width), up)
            down = jnp.where(mine, rolled(both, start), down)
    outer_ref[0:CX, :], inner_ref[0:CX, :] = in_order("gy", down, up)


def in_share(lane, start, width):
    inside = jnp.zeros(lane.shape, jnp.bool_)
    for level in range(LEV):
        first = CENTRE[level] + start
        inside = inside | ((lane >= first) & (lane < first + width))
    return inside


def pack_ends(outer_side, inner_side, vel_ref, seed_ref, cou_ref, vis_ref, outer_ref, inner_ref):
    def put(at, rows, down, up):
        span = pl.ds(at, rows)
        outer_ref[span, :], inner_ref[span, :] = in_order("gx", down, up)
        return at + rows

    at = 0
    for ref in (vel_ref, cou_ref, vis_ref):
        for level in range(LEV):
            at = put(at, RIM, ref[level, 0:RIM, :], ref[level, CX - RIM : CX, :])
    for level in range(LEV):
        at = put(at, THIN, seed_ref[level, 0:THIN, :], seed_ref[level, CX - THIN : CX, :])
    down = in_order("gy", outer_side[0:RIM, :], inner_side[0:RIM, :])
    up = in_order("gy", outer_side[CX - RIM : CX, :], inner_side[CX - RIM : CX, :])
    for side in range(2):
        at = put(at, RIM, down[side], up[side])
    last = SIDE_ROWS - THIN
    down = in_order("gy", outer_side[CX : CX + THIN, :], inner_side[CX : CX + THIN, :])
    up = in_order("gy", outer_side[last:SIDE_ROWS, :], inner_side[last:SIDE_ROWS, :])
    for side in range(2):
        at = put(at, THIN, down[side], up[side])


def level_mix(level):
    return VERTICAL_MIX * (2 if level == 1 else 1)


def rim_mixes():
    level_of, place = rim_place(lane_ids())
    valid = (place >= -WIDE) & (place < WIDE)
    upper = jnp.where(valid & (level_of != 2), VERTICAL_MIX, 0.0).astype(jnp.float32)
    lower = jnp.where(valid & (level_of != 0), VERTICAL_MIX, 0.0).astype(jnp.float32)
    return valid, upper, lower


def put_coefficients(bufs, tile, to, rows, courant, viscosity, mix):
    a_buf, w_buf, v_buf = bufs
    a_buf[tile, pl.ds(to, rows), :] = 1.0 - courant - 4.0 * viscosity - mix
    w_buf[tile, pl.ds(to, rows), :] = courant + viscosity
    v_buf[tile, pl.ds(to, rows), :] = viscosity


def put_rim(u_buf, bufs, west, east, to, rows):
    _, place = rim_place(lane_ids())
    _, upper, lower = rim_mixes()
    zero = jnp.zeros((rows, CY), jnp.float32)
    start = 0
    found = []
    for width in (WIDE, MID, MID):
        value = jnp.where((place >= 0) & (place < width), rolled(east, -start), zero)
        found.append(
            jnp.where((place >= -width) & (place < 0), rolled(west, -start - width), value)
        )
        start += width
    u_buf[LEV, pl.ds(to, rows), :] = found[0]
    put_coefficients(bufs, LEV, to, rows, found[1], found[2], upper + lower)


def put_thin_rim(l_buf, west, east, block, to, rows):
    level_of, place = rim_place(lane_ids())
    value = jnp.zeros((rows, CY), jnp.float32)
    for level in range(LEV):
        at = CENTRE[level] - (32 * block + THIN * level)
        mine = level_of == level
        value = jnp.where(mine & (place >= 0) & (place < THIN), rolled(east, at), value)
        value = jnp.where(mine & (place >= -THIN) & (place < 0), rolled(west, at - THIN), value)
    l_buf[LEV, pl.ds(to, rows), :] = value


def prepare(
    n_gx, n_gy, per_device,
    place_ref, info_ref, vel_ref, seed_ref, cou_ref, vis_ref, outer_side, inner_side,
    u_buf, l_buf, a_buf, w_buf, v_buf, d_buf, rows_buf, cols_buf,
):
    lane = lane_ids()
    level_of, place = rim_place(lane)
    level_one = level_of == 1
    valid, _, _ = rim_mixes()

    devices = info_ref.shape[0]
    my_gx = place_ref[0].astype(jnp.float32)
    my_gy = place_ref[1].astype(jnp.float32)
    col_of = jnp.where(place < 0, place, CY + place).astype(jnp.float32)
    row_lane = lax.broadcasted_iota(jnp.int32, (1, 3 * CY), 1).astype(jnp.float32)
    row_profiles, rim_profiles = [], []

    def near(delta, count):
        delta = jnp.where(delta >= count / 2, delta - count, delta)
        return jnp.where(delta < -count / 2, delta + count, delta)

    def profile(cells, first, width):
        at = cells - first
        centred = at - (FP - 1) / 2.0
        value = jnp.exp(-(centred * centred) / (2.0 * width * width))
        return jnp.where((at >= 0.0) & (at < float(FP)), value, 0.0)

    for k in range(per_device):
        info = info_ref[:, VALUES * k : VALUES * k + VALUES]
        row_first = near(info[:, 0:1] - my_gx, n_gx) * CX + info[:, 2:3]
        col_first = near(info[:, 1:2] - my_gy, n_gy) * CY + info[:, 3:4]
        scale = DRAG_SCALE * info[:, 4:5]
        width = info[:, 5:6]
        part = pl.ds(k * devices, devices)
        row_profiles.append(profile(row_lane - RIM, row_first, width) * scale)
        rows_buf[part, :] = profile(row_lane[:, :CX], row_first, width) * scale
        cols_buf[part, :] = profile(lane.astype(jnp.float32), col_first, width)
        rim_profiles.append(profile(col_of, col_first, width))
    along_rows = jnp.concatenate(row_profiles, axis=0)
    along_cols = jnp.concatenate([cols_buf[...], jnp.concatenate(rim_profiles, axis=0)], axis=1)
    drag = lax.dot_general(
        along_rows.T, along_cols, (((1,), (0,)), ((), ())),
        precision=lax.Precision.HIGHEST, preferred_element_type=jnp.float32,
    )
    tall = pl.ds(TOP - RIM, CX + 2 * RIM)
    gain = jnp.where(valid, jnp.where(level_one, 1.0, SIDE_GAIN), 0.0).astype(jnp.float32)
    d_buf[0, tall, :] = drag[: CX + 2 * RIM, :CY]
    d_buf[1, tall, :] = drag[: CX + 2 * RIM, :CY] * SIDE_GAIN
    d_buf[2, tall, :] = drag[: CX + 2 * RIM, CY:] * gain

    edge = jnp.zeros((TOP - RIM, CY), jnp.float32)
    for tile in range(LEV + 1):
        for buf in (a_buf, w_buf, v_buf, u_buf, l_buf):
            buf[tile, 0 : TOP - RIM, :] = edge
            buf[tile, TALL - TOP + RIM :, :] = edge
        l_buf[tile, TOP - RIM : TOP - THIN, :] = edge
        l_buf[tile, TOP + CX + THIN : TOP + CX + RIM, :] = edge
    inside = pl.ds(TOP, CX)
    bufs = (a_buf, w_buf, v_buf)
    for level in range(LEV):
        u_buf[level, inside, :] = vel_ref[level]
        l_buf[level, inside, :] = seed_ref[level]
        put_coefficients(bufs, level, TOP, CX, cou_ref[level], vis_ref[level], level_mix(level))
    west, east = in_order("gy", outer_side[...], inner_side[...])
    put_rim(u_buf, bufs, west[0:CX], east[0:CX], TOP, CX)
    for block in range(4):
        put_thin_rim(l_buf, west[CX:], east[CX:], block, TOP + 64 * block, 64)


def window(
    per_device,
    u_even_in, l_even_in, a_in, w_in, v_in, d_buf, rows_buf, cols_buf, outer_end, inner_end,
    start_ref, grads_ref, u_even, l_even, a_buf, w_buf, v_buf,
    u_odd, l_odd, g_buf, f_buf, s_buf, v_turned,
):
    u_buf, l_buf = (u_even, u_odd), (l_even, l_odd)
    bufs = (a_buf, w_buf, v_buf)
    lane = lane_ids()
    level_of, place = rim_place(lane)
    west_lane, east_lane = place == -1, place == 0
    level_zero, level_two = level_of == 0, level_of == 2
    _, upper, lower = rim_mixes()
    first_lane, last_lane = lane == 0, lane == CY - 1
    devices = grads_ref.shape[0]

    edge = jnp.zeros((TOP - RIM, CY), jnp.float32)
    for tile in range(LEV + 1):
        for buf in (u_odd, l_odd):
            buf[tile, 0 : TOP - RIM, :] = edge
            buf[tile, TALL - TOP + RIM :, :] = edge
        l_odd[tile, TOP - RIM : TOP - THIN, :] = edge
        l_odd[tile, TOP + CX + THIN : TOP + CX + RIM, :] = edge
    low_end, high_end = in_order("gx", outer_end[...], inner_end[...])
    for ref, to, thin_to, block in (
        (low_end, TOP - RIM, TOP - THIN, 3),
        (high_end, TOP + CX, TOP + CX, 0),
    ):
        for level in range(LEV):
            u_even[level, to : to + RIM, :] = ref[RIM * level : RIM * level + RIM]
            courant = ref[RIM * (LEV + level) : RIM * (LEV + level) + RIM]
            viscosity = ref[RIM * (2 * LEV + level) : RIM * (2 * LEV + level) + RIM]
            put_coefficients(bufs, level, to, RIM, courant, viscosity, level_mix(level))
            at = 3 * LEV * RIM + THIN * level
            l_even[level, thin_to : thin_to + THIN, :] = ref[at : at + THIN]
        at = 3 * LEV * RIM + LEV * THIN
        put_rim(u_even, bufs, ref[at : at + RIM], ref[at + RIM : at + 2 * RIM], to, RIM)
        at += 2 * RIM
        west, east = ref[at : at + THIN], ref[at + THIN : at + 2 * THIN]
        put_thin_rim(l_even, west, east, block, thin_to, THIN)

    def beyond(packed):
        return rolled(packed, GAP), rolled(packed, -GAP)

    def outward(tiles):
        other = jnp.where(level_zero, rolled(tiles[0], -GAP), tiles[1])
        return jnp.where(level_two, rolled(tiles[2], GAP), other)

    def sideways(tiles, across, with_rim=True):
        sums = []
        for tile in range(LEV + 1 if with_rim else LEV):
            low, high = (west_lane, east_lane) if tile == LEV else (last_lane, first_lane)
            left = rolled(jnp.where(low, across[tile], tiles[tile]), 1)
            right = rolled(jnp.where(high, across[tile], tiles[tile]), -1)
            sums.append(left + right)
        return sums

    def upright(core):
        middle = VERTICAL_MIX * core[1]
        return [middle, VERTICAL_MIX * (core[0] + core[2]), middle]

    def rim_upright(plus, minus):
        return upper * minus + lower * plus

    for index, turned in enumerate(beyond(v_buf[LEV, TOP - 8 : TOP + CX + 8, :])):
        v_turned[index, TOP - 8 : TOP + CX + 8, :] = turned

    def drag_of(tile, at):
        return d_buf[(1, 0, 1, 2)[tile], at, :]

    def drag_terms(state, drag_here):
        square = state * state + 1.0
        root = lax.rsqrt(square)
        weak = drag_here * root
        return square, root, weak, weak * square

    def staged(first, count, stages):
        chunks = [(first + at, min(CHUNK, count - at)) for at in range(0, count, CHUNK)]
        held = [None] * len(chunks)
        delay = (len(stages) - 1) * AHEAD
        for tick in range(len(chunks) + delay):
            for index, stage in enumerate(stages):
                at = tick - index * AHEAD
                if 0 <= at < len(chunks):
                    held[at] = stage(pl.ds(*chunks[at]), chunks[at], held[at])

    for step in range(STEPS - 1):
        rows_beyond = RIM if STEPS + 5 - step > 8 else 8
        now, later = step % 2, (step + 1) % 2

        def exchange(at, chunk, _, now=now):
            state = [u_buf[now][tile, at, :] for tile in range(LEV + 1)]
            return *beyond(state[LEV]), outward(state)

        def shift(at, chunk, held, now=now):
            plus, minus, other = held
            state = [u_buf[now][tile, at, :] for tile in range(LEV + 1)]
            return sideways(state, (plus, state[LEV], minus, other)), rim_upright(plus, minus)

        def advance(at, chunk, shifted, step=step, now=now, later=later):
            first, rows = chunk
            sides, mixed_rim = shifted
            state = [u_buf[now][tile, at, :] for tile in range(LEV + 1)]
            mixed = upright(state) + [mixed_rim]
            for tile in range(LEV + 1):
                upwind = u_buf[now][tile, pl.ds(first - 1, rows), :]
                downwind = u_buf[now][tile, pl.ds(first + 1, rows), :]
                square, root, weak, strong = drag_terms(state[tile], drag_of(tile, at))
                centre = a_buf[tile, at, :] - strong
                u_buf[later][tile, at, :] = (
                    centre * state[tile]
                    + w_buf[tile, at, :] * upwind
                    + v_buf[tile, at, :] * (downwind + sides[tile])
                    + mixed[tile]
                )
                g_buf[step, tile, at, :] = centre - strong + weak
                if tile < LEV:
                    f_buf[step, tile, at, :] = state[tile] * (square * root)

        staged(TOP - rows_beyond, CX + 2 * rows_beyond, (exchange, shift, advance))

    last = STEPS - 1

    def slopes(first, rows):
        at = pl.ds(first, rows)
        for tile in range(LEV + 1):
            state = u_buf[last % 2][tile, at, :]
            square, root, weak, strong = drag_terms(state, drag_of(tile, at))
            g_buf[last, tile, at, :] = a_buf[tile, at, :] - 2.0 * strong + weak
            if tile < LEV:
                f_buf[last, tile, at, :] = state * (square * root)

    for_rows(TOP - 8, CX + 16, CX + 16, slopes)

    zero = jnp.zeros((CX + 16, CY), jnp.float32)
    for part in range(2):
        s_buf[part, TOP - 8 : TOP + CX + 8, :] = zero
    for step in reversed(range(STEPS)):
        rows_beyond = 8 if step else 0
        now, later = (last - step) % 2, (last - step + 1) % 2

        def fluxes(at, now=now):
            adjoint = [l_buf[now][tile, at, :] for tile in range(LEV + 1)]
            return adjoint, [v_buf[tile, at, :] * adjoint[tile] for tile in range(LEV + 1)]

        def exchange(at, chunk, _, fluxes=fluxes):
            adjoint, flux = fluxes(at)
            return *beyond(adjoint[LEV]), outward(flux)

        def shift(at, chunk, held, fluxes=fluxes, step=step):
            plus, minus, other = held
            flux = fluxes(at)[1]
            across = plus * v_turned[0, at, :], flux[LEV], minus * v_turned[1, at, :], other
            return sideways(flux, across, bool(step)), rim_upright(plus, minus) if step else None

        def retreat(at, chunk, shifted, step=step, now=now, later=later):
            first, rows = chunk
            sides, mixed_rim = shifted
            before, after = pl.ds(first - 1, rows), pl.ds(first + 1, rows)
            adjoint = [l_buf[now][tile, at, :] for tile in range(LEV + 1)]
            mixed = upright(adjoint) + [mixed_rim]
            for tile in range(LEV + 1 if step else LEV):
                value = (
                    g_buf[step, tile, at, :] * adjoint[tile]
                    + w_buf[tile, after, :] * l_buf[now][tile, after, :]
                    + v_buf[tile, before, :] * l_buf[now][tile, before, :]
                    + sides[tile]
                    + mixed[tile]
                )
                if step:
                    l_buf[later][tile, at, :] = value
                else:
                    start_ref[tile, pl.ds(first - TOP, rows), :] = value
            s_buf[0, at, :] += f_buf[step, 1, at, :] * adjoint[1]
            s_buf[1, at, :] += (
                f_buf[step, 0, at, :] * adjoint[0] + f_buf[step, 2, at, :] * adjoint[2]
            )

        staged(TOP - rows_beyond, CX + 2 * rows_beyond, (exchange, shift, retreat))

    inside = pl.ds(TOP, CX)
    sensitivity = s_buf[0, inside, :] + SIDE_GAIN * s_buf[1, inside, :]
    across = lax.dot_general(
        rows_buf[...], sensitivity, (((1,), (0,)), ((), ())),
        precision=lax.Precision.HIGHEST, preferred_element_type=jnp.float32,
    )
    sums = -jnp.sum(across * cols_buf[...], axis=1, keepdims=True)
    grads = jnp.zeros((devices, CY), jnp.float32)
    for k in range(per_device):
        mine = spread_lanes(sums[k * devices : (k + 1) * devices, :], devices)
        grads = jnp.where(lane == k, mine, grads)
    grads_ref[...] = grads


def shards(
    velocity, adjoint_seed, courant, viscosity, turbine_tile, turbine_offset, thrust, disk_width
):
    n_gx, n_gy = lax.axis_size("gx"), lax.axis_size("gy")
    devices = n_gx * n_gy
    per_device = thrust.shape[0]
    f32 = jnp.float32
    vmem = pl.BlockSpec(memory_space=pltpu.VMEM)

    def swap(axis, array, odd_up):
        count = lax.axis_size(axis)
        step = 1 if odd_up else -1
        return lax.ppermute(
            array, axis, [(i, (i + (step if i % 2 else -step)) % count) for i in range(count)]
        )

    outer, inner, info = pl.pallas_call(
        functools.partial(pack_sides, n_gy),
        name="pack_sides",
        out_shape=(
            jax.ShapeDtypeStruct((SIDE_ROWS, CY), f32),
            jax.ShapeDtypeStruct((SIDE_ROWS, CY), f32),
            jax.ShapeDtypeStruct((devices, CY), f32),
        ),
        in_specs=[pl.BlockSpec(memory_space=pl.ANY)] * 8,
        out_specs=(vmem,) * 3,
        scratch_shapes=[
            pltpu.SMEM((per_device,), jnp.int32),
            pltpu.SMEM((2, per_device), jnp.int32),
            pltpu.SMEM((per_device,), f32),
            pltpu.SMEM((per_device,), f32),
            *[pltpu.VMEM((LEV, CX, CY), f32)] * 4,
            pltpu.SemaphoreType.DMA((8,)),
        ],
    )(turbine_tile.reshape(per_device), turbine_offset.T, thrust, disk_width, velocity, adjoint_seed, courant, viscosity)
    outer_side, inner_side = swap("gy", outer, True), swap("gy", inner, False)
    info = lax.all_to_all(info, ("gx", "gy"), 0, 0, tiled=True)
    outer, inner = pl.pallas_call(
        pack_ends,
        name="pack_ends",
        out_shape=(jax.ShapeDtypeStruct((END_ROWS, CY), f32),) * 2,
        in_specs=[vmem] * 6,
        out_specs=(vmem,) * 2,
        compiler_params=SMALL,
    )(outer_side, inner_side, velocity, adjoint_seed, courant, viscosity)
    outer_end, inner_end = swap("gx", outer, True), swap("gx", inner, False)
    place = jnp.stack([lax.axis_index("gx"), lax.axis_index("gy")]).astype(jnp.int32)
    turbines = devices * per_device
    field = jax.ShapeDtypeStruct((LEV + 1, TALL, CY), f32)
    fields = pl.pallas_call(
        functools.partial(prepare, n_gx, n_gy, per_device),
        name="prepare",
        out_shape=(
            *[field] * 5,
            jax.ShapeDtypeStruct((3, TALL, CY), f32),
            jax.ShapeDtypeStruct((turbines, CX), f32),
            jax.ShapeDtypeStruct((turbines, CY), f32),
        ),
        in_specs=[pl.BlockSpec(memory_space=pltpu.SMEM)] + [vmem] * 7,
        out_specs=(vmem,) * 8,
        compiler_params=SMALL,
        cost_estimate=pl.CostEstimate(flops=40000000, bytes_accessed=8000000, transcendentals=0),
    )(place, info, velocity, adjoint_seed, courant, viscosity, outer_side, inner_side)
    adjoint_start, grads, *_ = pl.pallas_call(
        functools.partial(window, per_device),
        name="window",
        out_shape=(
            jax.ShapeDtypeStruct((LEV, CX, CY), f32),
            jax.ShapeDtypeStruct((devices, CY), f32),
            *[field] * 5,
        ),
        in_specs=[vmem] * 10,
        out_specs=(vmem,) * 7,
        input_output_aliases={index: index + 2 for index in range(5)},
        scratch_shapes=[
            pltpu.VMEM((LEV + 1, TALL, CY), f32),
            pltpu.VMEM((LEV + 1, TALL, CY), f32),
            pltpu.VMEM((STEPS, LEV + 1, TALL, CY), f32),
            pltpu.VMEM((STEPS, LEV, TALL, CY), f32),
            pltpu.VMEM((2, TALL, CY), f32),
            pltpu.VMEM((2, TALL, CY), f32),
        ],
        compiler_params=pltpu.CompilerParams(vmem_limit_bytes=24 * 1024 * 1024),
    )(*fields, outer_end, inner_end)
    grads = lax.all_to_all(grads, ("gx", "gy"), 0, 0, tiled=True)
    return adjoint_start, jnp.sum(grads, axis=0)[:per_device]


def solution(mesh):
    tiled = P(None, "gx", "gy")
    spread = P(("gx", "gy"))
    matrix = P(("gx", "gy"), None)
    return jax.shard_map(
        shards,
        mesh=mesh,
        in_specs=(tiled, tiled, tiled, tiled, matrix, matrix, spread, spread),
        out_specs=(tiled, spread),
        check_vma=False,
    )
```

```python
import functools
import math

import jax
import jax.numpy as jnp
from jax import lax
from jax.experimental import pallas as pl
from jax.experimental.pallas import tpu as pltpu
from jax.sharding import PartitionSpec as P

STEPS = 8
FP = 64
VERTICAL_MIX = 0.05
DRAG_SCALE = 0.01
SIDE_GAIN = math.exp(-0.5)

LEV, CX, CY = 3, 256, 128
WIDE = 14
MID = 13
THIN = 8
GAP = 42
CENTRE = (CY - GAP, 0, GAP)
RIM = 16
TOP = 24
TALL = CX + 2 * TOP
SIDE_ROWS = CX + 64
END_ROWS = 3 * LEV * RIM + LEV * THIN + 2 * RIM + 2 * THIN
VALUES = 6
CHUNK = 32
AHEAD = 2
SMALL = pltpu.CompilerParams(vmem_limit_bytes=8 * 1024 * 1024)


def lane_ids():
    return lax.broadcasted_iota(jnp.int32, (1, CY), 1)


def spread_lanes(value, rows):
    return jnp.broadcast_to(value, (rows, CY))


def rolled(value, shift):
    shift = shift % CY
    return value if shift == 0 else pltpu.roll(value, shift, 1)


def rim_place(lane):
    level = jnp.where((lane >= GAP // 2) & (lane < CY // 2), 2, 1)
    level = jnp.where((lane >= CY // 2) & (lane < CY - GAP // 2), 0, level)
    place = lane - jnp.where(level == 2, GAP, jnp.where(level == 0, CY - GAP, 0))
    place = jnp.where(lane >= CY - GAP // 2, lane - CY, place)
    return level, place


def for_rows(first, count, chunk, body):
    full = count // chunk
    if full == 1:
        body(first, chunk)
    elif full > 1:

        def one(index, carry):
            body(pl.multiple_of(first + index * chunk, 8), chunk)
            return carry

        lax.fori_loop(0, full, one, 0)
    if count > full * chunk:
        body(first + full * chunk, count - full * chunk)


def is_odd(axis):
    return lax.axis_index(axis) % 2 == 1


def in_order(axis, first, second):
    odd = is_odd(axis)
    return jnp.where(odd, second, first), jnp.where(odd, first, second)


def pack_sides(
    n_gy, tile_hbm, offset_hbm, thrust_hbm, width_hbm, vel_hbm, seed_hbm, cou_hbm, vis_hbm,
    outer_ref, inner_ref, info_ref,
    tile_ref, offset_ref, thrust_ref, width_ref, vel_ref, seed_ref, cou_ref, vis_ref, arrived,
):
    copies = [
        pltpu.make_async_copy(source, target, arrived.at[index])
        for index, (source, target) in enumerate(
            (
                (seed_hbm, seed_ref), (vel_hbm, vel_ref), (cou_hbm, cou_ref), (vis_hbm, vis_ref),
                (tile_hbm, tile_ref), (offset_hbm, offset_ref), (thrust_hbm, thrust_ref),
                (width_hbm, width_ref),
            )
        )
    ]
    for copy in copies:
        copy.start()
    lane = lane_ids()
    level_of, _ = rim_place(lane)
    for copy in copies[4:]:
        copy.wait()
    whole = jnp.zeros((1, CY), jnp.int32)
    real = jnp.zeros((1, CY), jnp.float32)
    for k in range(thrust_ref.shape[0]):
        tile = tile_ref[k]
        for spot, value in enumerate(
            (tile // n_gy, tile % n_gy, offset_ref[0, k], offset_ref[1, k])
        ):
            whole = jnp.where(lane == VALUES * k + spot, value, whole)
        real = jnp.where(lane == VALUES * k + 4, thrust_ref[k], real)
        real = jnp.where(lane == VALUES * k + 5, width_ref[k], real)
    info_ref[...] = jnp.broadcast_to(whole.astype(jnp.float32) + real, info_ref.shape)

    copies[0].wait()
    thin = []
    for low in (True, False):
        total = jnp.zeros((64, CY), jnp.float32)
        for block in range(4):
            for level in range(LEV):
                to = 32 * block + THIN * level
                moved = rolled(
                    seed_ref[level, 64 * block : 64 * block + 64, :],
                    to - (0 if low else CY - THIN),
                )
                total = jnp.where((lane >= to) & (lane < to + THIN), moved, total)
        thin.append(total)
    outer_ref[CX:SIDE_ROWS, :], inner_ref[CX:SIDE_ROWS, :] = in_order("gy", *thin)

    def around(ref):
        value = jnp.where(level_of == 0, rolled(ref[0], -GAP), ref[1])
        return jnp.where(level_of == 2, rolled(ref[2], GAP), value)

    up = down = None
    for index, (ref, width) in enumerate(((vel_ref, WIDE), (cou_ref, MID), (vis_ref, MID))):
        copies[1 + index].wait()
        both = around(ref)
        start = (0, WIDE, WIDE + MID)[index]
        if index == 0:
            up, down = rolled(both, width), both
        else:
            mine = in_share(lane, start, width)
            up = jnp.where(mine, rolled(both, start + width), up)
            down = jnp.where(mine, rolled(both, start), down)
    outer_ref[0:CX, :], inner_ref[0:CX, :] = in_order("gy", down, up)


def in_share(lane, start, width):
    inside = jnp.zeros(lane.shape, jnp.bool_)
    for level in range(LEV):
        first = CENTRE[level] + start
        inside = inside | ((lane >= first) & (lane < first + width))
    return inside


def pack_ends(outer_side, inner_side, vel_ref, seed_ref, cou_ref, vis_ref, outer_ref, inner_ref):
    def put(at, rows, down, up):
        span = pl.ds(at, rows)
        outer_ref[span, :], inner_ref[span, :] = in_order("gx", down, up)
        return at + rows

    at = 0
    for ref in (vel_ref, cou_ref, vis_ref):
        for level in range(LEV):
            at = put(at, RIM, ref[level, 0:RIM, :], ref[level, CX - RIM : CX, :])
    for level in range(LEV):
        at = put(at, THIN, seed_ref[level, 0:THIN, :], seed_ref[level, CX - THIN : CX, :])
    down = in_order("gy", outer_side[0:RIM, :], inner_side[0:RIM, :])
    up = in_order("gy", outer_side[CX - RIM : CX, :], inner_side[CX - RIM : CX, :])
    for side in range(2):
        at = put(at, RIM, down[side], up[side])
    last = SIDE_ROWS - THIN
    down = in_order("gy", outer_side[CX : CX + THIN, :], inner_side[CX : CX + THIN, :])
    up = in_order("gy", outer_side[last:SIDE_ROWS, :], inner_side[last:SIDE_ROWS, :])
    for side in range(2):
        at = put(at, THIN, down[side], up[side])


def level_mix(level):
    return VERTICAL_MIX * (2 if level == 1 else 1)


def rim_mixes():
    level_of, place = rim_place(lane_ids())
    valid = (place >= -WIDE) & (place < WIDE)
    upper = jnp.where(valid & (level_of != 2), VERTICAL_MIX, 0.0).astype(jnp.float32)
    lower = jnp.where(valid & (level_of != 0), VERTICAL_MIX, 0.0).astype(jnp.float32)
    return valid, upper, lower


def put_coefficients(bufs, tile, to, rows, courant, viscosity, mix):
    a_buf, w_buf, v_buf = bufs
    a_buf[tile, pl.ds(to, rows), :] = 1.0 - courant - 4.0 * viscosity - mix
    w_buf[tile, pl.ds(to, rows), :] = courant + viscosity
    v_buf[tile, pl.ds(to, rows), :] = viscosity


def put_rim(u_buf, bufs, west, east, to, rows):
    _, place = rim_place(lane_ids())
    _, upper, lower = rim_mixes()
    zero = jnp.zeros((rows, CY), jnp.float32)
    start = 0
    found = []
    for width in (WIDE, MID, MID):
        value = jnp.where((place >= 0) & (place < width), rolled(east, -start), zero)
        found.append(
            jnp.where((place >= -width) & (place < 0), rolled(west, -start - width), value)
        )
        start += width
    u_buf[LEV, pl.ds(to, rows), :] = found[0]
    put_coefficients(bufs, LEV, to, rows, found[1], found[2], upper + lower)


def put_thin_rim(l_buf, west, east, block, to, rows):
    level_of, place = rim_place(lane_ids())
    value = jnp.zeros((rows, CY), jnp.float32)
    for level in range(LEV):
        at = CENTRE[level] - (32 * block + THIN * level)
        mine = level_of == level
        value = jnp.where(mine & (place >= 0) & (place < THIN), rolled(east, at), value)
        value = jnp.where(mine & (place >= -THIN) & (place < 0), rolled(west, at - THIN), value)
    l_buf[LEV, pl.ds(to, rows), :] = value


def prepare(
    n_gx, n_gy, per_device,
    place_ref, info_ref, vel_ref, seed_ref, cou_ref, vis_ref, outer_side, inner_side,
    u_buf, l_buf, a_buf, w_buf, v_buf, d_buf, rows_buf, cols_buf,
):
    lane = lane_ids()
    level_of, place = rim_place(lane)
    level_one = level_of == 1
    valid, _, _ = rim_mixes()

    devices = info_ref.shape[0]
    my_gx = place_ref[0].astype(jnp.float32)
    my_gy = place_ref[1].astype(jnp.float32)
    col_of = jnp.where(place < 0, place, CY + place).astype(jnp.float32)
    row_lane = lax.broadcasted_iota(jnp.int32, (1, 3 * CY), 1).astype(jnp.float32)
    row_profiles, rim_profiles = [], []

    def near(delta, count):
        delta = jnp.where(delta >= count / 2, delta - count, delta)
        return jnp.where(delta < -count / 2, delta + count, delta)

    def profile(cells, first, width):
        at = cells - first
        centred = at - (FP - 1) / 2.0
        value = jnp.exp(-(centred * centred) / (2.0 * width * width))
        return jnp.where((at >= 0.0) & (at < float(FP)), value, 0.0)

    for k in range(per_device):
        info = info_ref[:, VALUES * k : VALUES * k + VALUES]
        row_first = near(info[:, 0:1] - my_gx, n_gx) * CX + info[:, 2:3]
        col_first = near(info[:, 1:2] - my_gy, n_gy) * CY + info[:, 3:4]
        scale = DRAG_SCALE * info[:, 4:5]
        width = info[:, 5:6]
        part = pl.ds(k * devices, devices)
        row_profiles.append(profile(row_lane - RIM, row_first, width) * scale)
        rows_buf[part, :] = profile(row_lane[:, :CX], row_first, width) * scale
        cols_buf[part, :] = profile(lane.astype(jnp.float32), col_first, width)
        rim_profiles.append(profile(col_of, col_first, width))
    along_rows = jnp.concatenate(row_profiles, axis=0)
    along_cols = jnp.concatenate([cols_buf[...], jnp.concatenate(rim_profiles, axis=0)], axis=1)
    drag = lax.dot_general(
        along_rows.T, along_cols, (((1,), (0,)), ((), ())),
        precision=lax.Precision.HIGHEST, preferred_element_type=jnp.float32,
    )
    tall = pl.ds(TOP - RIM, CX + 2 * RIM)
    gain = jnp.where(valid, jnp.where(level_one, 1.0, SIDE_GAIN), 0.0).astype(jnp.float32)
    d_buf[0, tall, :] = drag[: CX + 2 * RIM, :CY]
    d_buf[1, tall, :] = drag[: CX + 2 * RIM, :CY] * SIDE_GAIN
    d_buf[2, tall, :] = drag[: CX + 2 * RIM, CY:] * gain

    edge = jnp.zeros((TOP - RIM, CY), jnp.float32)
    for tile in range(LEV + 1):
        for buf in (a_buf, w_buf, v_buf, u_buf, l_buf):
            buf[tile, 0 : TOP - RIM, :] = edge
            buf[tile, TALL - TOP + RIM :, :] = edge
        l_buf[tile, TOP - RIM : TOP - THIN, :] = edge
        l_buf[tile, TOP + CX + THIN : TOP + CX + RIM, :] = edge
    inside = pl.ds(TOP, CX)
    bufs = (a_buf, w_buf, v_buf)
    for level in range(LEV):
        u_buf[level, inside, :] = vel_ref[level]
        l_buf[level, inside, :] = seed_ref[level]
        put_coefficients(bufs, level, TOP, CX, cou_ref[level], vis_ref[level], level_mix(level))
    west, east = in_order("gy", outer_side[...], inner_side[...])
    put_rim(u_buf, bufs, west[0:CX], east[0:CX], TOP, CX)
    for block in range(4):
        put_thin_rim(l_buf, west[CX:], east[CX:], block, TOP + 64 * block, 64)


def window(
    per_device,
    u_even_in, l_even_in, a_in, w_in, v_in, d_buf, rows_buf, cols_buf, outer_end, inner_end,
    start_ref, grads_ref, u_even, l_even, a_buf, w_buf, v_buf,
    u_odd, l_odd, g_buf, f_buf, s_buf, v_turned, turns,
):
    u_buf, l_buf = (u_even, u_odd), (l_even, l_odd)
    bufs = (a_buf, w_buf, v_buf)
    lane = lane_ids()
    level_of, place = rim_place(lane)
    west_lane, east_lane = place == -1, place == 0
    level_zero, level_two = level_of == 0, level_of == 2
    _, upper, lower = rim_mixes()
    first_lane, last_lane = lane == 0, lane == CY - 1
    devices = grads_ref.shape[0]

    edge = jnp.zeros((TOP - RIM, CY), jnp.float32)
    for tile in range(LEV + 1):
        for buf in (u_odd, l_odd):
            buf[tile, 0 : TOP - RIM, :] = edge
            buf[tile, TALL - TOP + RIM :, :] = edge
        l_odd[tile, TOP - RIM : TOP - THIN, :] = edge
        l_odd[tile, TOP + CX + THIN : TOP + CX + RIM, :] = edge
    low_end, high_end = in_order("gx", outer_end[...], inner_end[...])
    for ref, to, thin_to, block in (
        (low_end, TOP - RIM, TOP - THIN, 3),
        (high_end, TOP + CX, TOP + CX, 0),
    ):
        for level in range(LEV):
            u_even[level, to : to + RIM, :] = ref[RIM * level : RIM * level + RIM]
            courant = ref[RIM * (LEV + level) : RIM * (LEV + level) + RIM]
            viscosity = ref[RIM * (2 * LEV + level) : RIM * (2 * LEV + level) + RIM]
            put_coefficients(bufs, level, to, RIM, courant, viscosity, level_mix(level))
            at = 3 * LEV * RIM + THIN * level
            l_even[level, thin_to : thin_to + THIN, :] = ref[at : at + THIN]
        at = 3 * LEV * RIM + LEV * THIN
        put_rim(u_even, bufs, ref[at : at + RIM], ref[at + RIM : at + 2 * RIM], to, RIM)
        at += 2 * RIM
        west, east = ref[at : at + THIN], ref[at + THIN : at + 2 * THIN]
        put_thin_rim(l_even, west, east, block, thin_to, THIN)

    def beyond(packed):
        high = packed.astype(jnp.bfloat16)
        low = (packed - high.astype(jnp.float32)).astype(jnp.bfloat16)
        both = lax.dot_general(
            jnp.concatenate([high, low], axis=1), turns[...], (((1,), (0,)), ((), ())),
            preferred_element_type=jnp.float32,
        )
        return both[:, :CY], both[:, CY:]

    def whole_turned(buf, rows_beyond):
        first = TOP - rows_beyond
        plus, minus = beyond(buf[LEV, first : TOP + CX + rows_beyond, :])
        return first, plus, minus

    def cut(turned, chunk):
        first, plus, minus = turned
        at, rows = chunk[0] - first, chunk[1]
        return plus[at : at + rows], minus[at : at + rows]

    def outward(tiles):
        other = jnp.where(level_zero, rolled(tiles[0], -GAP), tiles[1])
        return jnp.where(level_two, rolled(tiles[2], GAP), other)

    def sideways(tiles, across, with_rim=True):
        sums = []
        for tile in range(LEV + 1 if with_rim else LEV):
            low, high = (west_lane, east_lane) if tile == LEV else (last_lane, first_lane)
            left = rolled(jnp.where(low, across[tile], tiles[tile]), 1)
            right = rolled(jnp.where(high, across[tile], tiles[tile]), -1)
            sums.append(left + right)
        return sums

    def upright(core):
        middle = VERTICAL_MIX * core[1]
        return [middle, VERTICAL_MIX * (core[0] + core[2]), middle]

    def rim_upright(plus, minus):
        return upper * minus + lower * plus

    source = lax.broadcasted_iota(jnp.int32, (2 * CY, 2 * CY), 0) % CY
    target = lax.broadcasted_iota(jnp.int32, (2 * CY, 2 * CY), 1)
    wanted = (target % CY + jnp.where(target < CY, CY - GAP, GAP)) % CY
    turns[...] = jnp.where(source == wanted, 1.0, 0.0).astype(jnp.bfloat16)
    rim_spread = v_buf[LEV, TOP - 8 : TOP + CX + 8, :]
    for index, turned in enumerate((rolled(rim_spread, GAP), rolled(rim_spread, -GAP))):
        v_turned[index, TOP - 8 : TOP + CX + 8, :] = turned

    def drag_of(tile, at):
        return d_buf[(1, 0, 1, 2)[tile], at, :]

    def drag_terms(state, drag_here):
        square = state * state + 1.0
        root = lax.rsqrt(square)
        weak = drag_here * root
        return square, root, weak, weak * square

    def staged(first, count, stages):
        chunks = [(first + at, min(CHUNK, count - at)) for at in range(0, count, CHUNK)]
        held = [None] * len(chunks)
        delay = (len(stages) - 1) * AHEAD
        for tick in range(len(chunks) + delay):
            for index, stage in enumerate(stages):
                at = tick - index * AHEAD
                if 0 <= at < len(chunks):
                    held[at] = stage(pl.ds(*chunks[at]), chunks[at], held[at])

    for step in range(STEPS - 1):
        rows_beyond = RIM if STEPS + 5 - step > 8 else 8
        now, later = step % 2, (step + 1) % 2

        turned = whole_turned(u_buf[now], rows_beyond)

        def exchange(at, chunk, _, now=now, turned=turned):
            state = [u_buf[now][tile, at, :] for tile in range(LEV + 1)]
            return *cut(turned, chunk), outward(state)

        def shift(at, chunk, held, now=now):
            plus, minus, other = held
            state = [u_buf[now][tile, at, :] for tile in range(LEV + 1)]
            return sideways(state, (plus, state[LEV], minus, other)), rim_upright(plus, minus)

        def advance(at, chunk, shifted, step=step, now=now, later=later):
            first, rows = chunk
            sides, mixed_rim = shifted
            state = [u_buf[now][tile, at, :] for tile in range(LEV + 1)]
            mixed = upright(state) + [mixed_rim]
            for tile in range(LEV + 1):
                upwind = u_buf[now][tile, pl.ds(first - 1, rows), :]
                downwind = u_buf[now][tile, pl.ds(first + 1, rows), :]
                square, root, weak, strong = drag_terms(state[tile], drag_of(tile, at))
                centre = a_buf[tile, at, :] - strong
                u_buf[later][tile, at, :] = (
                    centre * state[tile]
                    + w_buf[tile, at, :] * upwind
                    + v_buf[tile, at, :] * (downwind + sides[tile])
                    + mixed[tile]
                )
                g_buf[step, tile, at, :] = centre - strong + weak
                if tile < LEV:
                    f_buf[step, tile, at, :] = state[tile] * (square * root)

        staged(TOP - rows_beyond, CX + 2 * rows_beyond, (exchange, shift, advance))

    last = STEPS - 1

    def slopes(first, rows):
        at = pl.ds(first, rows)
        for tile in range(LEV + 1):
            state = u_buf[last % 2][tile, at, :]
            square, root, weak, strong = drag_terms(state, drag_of(tile, at))
            g_buf[last, tile, at, :] = a_buf[tile, at, :] - 2.0 * strong + weak
            if tile < LEV:
                f_buf[last, tile, at, :] = state * (square * root)

    for_rows(TOP - 8, CX + 16, CX + 16, slopes)

    zero = jnp.zeros((CX + 16, CY), jnp.float32)
    for part in range(2):
        s_buf[part, TOP - 8 : TOP + CX + 8, :] = zero
    for step in reversed(range(STEPS)):
        rows_beyond = 8 if step else 0
        now, later = (last - step) % 2, (last - step + 1) % 2

        def fluxes(at, now=now):
            adjoint = [l_buf[now][tile, at, :] for tile in range(LEV + 1)]
            return adjoint, [v_buf[tile, at, :] * adjoint[tile] for tile in range(LEV + 1)]

        turned = whole_turned(l_buf[now], rows_beyond)

        def exchange(at, chunk, _, fluxes=fluxes, turned=turned):
            return *cut(turned, chunk), outward(fluxes(at)[1])

        def shift(at, chunk, held, fluxes=fluxes, step=step):
            plus, minus, other = held
            flux = fluxes(at)[1]
            across = plus * v_turned[0, at, :], flux[LEV], minus * v_turned[1, at, :], other
            return sideways(flux, across, bool(step)), rim_upright(plus, minus) if step else None

        def retreat(at, chunk, shifted, step=step, now=now, later=later):
            first, rows = chunk
            sides, mixed_rim = shifted
            before, after = pl.ds(first - 1, rows), pl.ds(first + 1, rows)
            adjoint = [l_buf[now][tile, at, :] for tile in range(LEV + 1)]
            mixed = upright(adjoint) + [mixed_rim]
            for tile in range(LEV + 1 if step else LEV):
                value = (
                    g_buf[step, tile, at, :] * adjoint[tile]
                    + w_buf[tile, after, :] * l_buf[now][tile, after, :]
                    + v_buf[tile, before, :] * l_buf[now][tile, before, :]
                    + sides[tile]
                    + mixed[tile]
                )
                if step:
                    l_buf[later][tile, at, :] = value
                else:
                    start_ref[tile, pl.ds(first - TOP, rows), :] = value
            s_buf[0, at, :] += f_buf[step, 1, at, :] * adjoint[1]
            s_buf[1, at, :] += (
                f_buf[step, 0, at, :] * adjoint[0] + f_buf[step, 2, at, :] * adjoint[2]
            )

        staged(TOP - rows_beyond, CX + 2 * rows_beyond, (exchange, shift, retreat))

    inside = pl.ds(TOP, CX)
    sensitivity = s_buf[0, inside, :] + SIDE_GAIN * s_buf[1, inside, :]
    across = lax.dot_general(
        rows_buf[...], sensitivity, (((1,), (0,)), ((), ())),
        precision=lax.Precision.HIGHEST, preferred_element_type=jnp.float32,
    )
    sums = -jnp.sum(across * cols_buf[...], axis=1, keepdims=True)
    grads = jnp.zeros((devices, CY), jnp.float32)
    for k in range(per_device):
        mine = spread_lanes(sums[k * devices : (k + 1) * devices, :], devices)
        grads = jnp.where(lane == k, mine, grads)
    grads_ref[...] = grads


def shards(
    velocity, adjoint_seed, courant, viscosity, turbine_tile, turbine_offset, thrust, disk_width
):
    n_gx, n_gy = lax.axis_size("gx"), lax.axis_size("gy")
    devices = n_gx * n_gy
    per_device = thrust.shape[0]
    f32 = jnp.float32
    vmem = pl.BlockSpec(memory_space=pltpu.VMEM)

    def swap(axis, array, odd_up):
        count = lax.axis_size(axis)
        step = 1 if odd_up else -1
        return lax.ppermute(
            array, axis, [(i, (i + (step if i % 2 else -step)) % count) for i in range(count)]
        )

    outer, inner, info = pl.pallas_call(
        functools.partial(pack_sides, n_gy),
        name="pack_sides",
        out_shape=(
            jax.ShapeDtypeStruct((SIDE_ROWS, CY), f32),
            jax.ShapeDtypeStruct((SIDE_ROWS, CY), f32),
            jax.ShapeDtypeStruct((devices, CY), f32),
        ),
        in_specs=[pl.BlockSpec(memory_space=pl.ANY)] * 8,
        out_specs=(vmem,) * 3,
        scratch_shapes=[
            pltpu.SMEM((per_device,), jnp.int32),
            pltpu.SMEM((2, per_device), jnp.int32),
            pltpu.SMEM((per_device,), f32),
            pltpu.SMEM((per_device,), f32),
            *[pltpu.VMEM((LEV, CX, CY), f32)] * 4,
            pltpu.SemaphoreType.DMA((8,)),
        ],
    )(turbine_tile.reshape(per_device), turbine_offset.T, thrust, disk_width, velocity, adjoint_seed, courant, viscosity)
    outer_side, inner_side = swap("gy", outer, True), swap("gy", inner, False)
    info = lax.all_to_all(info, ("gx", "gy"), 0, 0, tiled=True)
    outer, inner = pl.pallas_call(
        pack_ends,
        name="pack_ends",
        out_shape=(jax.ShapeDtypeStruct((END_ROWS, CY), f32),) * 2,
        in_specs=[vmem] * 6,
        out_specs=(vmem,) * 2,
        compiler_params=SMALL,
    )(outer_side, inner_side, velocity, adjoint_seed, courant, viscosity)
    outer_end, inner_end = swap("gx", outer, True), swap("gx", inner, False)
    place = jnp.stack([lax.axis_index("gx"), lax.axis_index("gy")]).astype(jnp.int32)
    turbines = devices * per_device
    field = jax.ShapeDtypeStruct((LEV + 1, TALL, CY), f32)
    fields = pl.pallas_call(
        functools.partial(prepare, n_gx, n_gy, per_device),
        name="prepare",
        out_shape=(
            *[field] * 5,
            jax.ShapeDtypeStruct((3, TALL, CY), f32),
            jax.ShapeDtypeStruct((turbines, CX), f32),
            jax.ShapeDtypeStruct((turbines, CY), f32),
        ),
        in_specs=[pl.BlockSpec(memory_space=pltpu.SMEM)] + [vmem] * 7,
        out_specs=(vmem,) * 8,
        compiler_params=SMALL,
        cost_estimate=pl.CostEstimate(flops=40000000, bytes_accessed=8000000, transcendentals=0),
    )(place, info, velocity, adjoint_seed, courant, viscosity, outer_side, inner_side)
    adjoint_start, grads, *_ = pl.pallas_call(
        functools.partial(window, per_device),
        name="window",
        out_shape=(
            jax.ShapeDtypeStruct((LEV, CX, CY), f32),
            jax.ShapeDtypeStruct((devices, CY), f32),
            *[field] * 5,
        ),
        in_specs=[vmem] * 10,
        out_specs=(vmem,) * 7,
        input_output_aliases={index: index + 2 for index in range(5)},
        scratch_shapes=[
            pltpu.VMEM((LEV + 1, TALL, CY), f32),
            pltpu.VMEM((LEV + 1, TALL, CY), f32),
            pltpu.VMEM((STEPS, LEV + 1, TALL, CY), f32),
            pltpu.VMEM((STEPS, LEV, TALL, CY), f32),
            pltpu.VMEM((2, TALL, CY), f32),
            pltpu.VMEM((2, TALL, CY), f32),
            pltpu.VMEM((2 * CY, 2 * CY), jnp.bfloat16),
        ],
        compiler_params=pltpu.CompilerParams(vmem_limit_bytes=24 * 1024 * 1024),
    )(*fields, outer_end, inner_end)
    grads = lax.all_to_all(grads, ("gx", "gy"), 0, 0, tiled=True)
    return adjoint_start, jnp.sum(grads, axis=0)[:per_device]


def solution(mesh):
    tiled = P(None, "gx", "gy")
    spread = P(("gx", "gy"))
    matrix = P(("gx", "gy"), None)
    return jax.shard_map(
        shards,
        mesh=mesh,
        in_specs=(tiled, tiled, tiled, tiled, matrix, matrix, spread, spread),
        out_specs=(tiled, spread),
        check_vma=False,
    )
```
